256 devices in a mesh: adapter: 32 (over z, x_hi, core), tensor: 8 (over y, x_lo).
Axes of the slice: x: 4 (x_hi: 2, x_lo: 2; x = x_hi * 2 + x_lo), y: 4, z: 8, core: 2. Of those that a mesh axis runs over, the one named last changes fastest.
Arguments:
- acts: bfloat16 [65536, 8192], P(('adapter', 'tensor')), may hold values from -6 to 6
- output_gradient: bfloat16 [65536, 1024], P(('adapter', 'tensor')), may hold values from -6 to 6
- adapter_middle_saved: bfloat16 [65536, 16], P(('adapter', 'tensor')), may hold values from -4 to 4
- adapter_per_row: int32 [65536], P(('adapter', 'tensor')), may hold values from 0 to 128, as said below
- segment_first_row: int32 [32, 13], P('adapter'), may hold values from 0 to 1920, as said below
- adapter_per_slot: int32 [32, 13], replicated, may hold values from 0 to 127, as said below
- adapter_storage_row: int32 [128], replicated, may hold values from 0 to 127, as said below
- frozen_value_weight: bfloat16 [8192, 1024], P('tensor'), may hold values from -0.1875 to 0.1875
- slot_down_matrix: bfloat16 [32, 13, 16, 8192], P('adapter', None, None, 'tensor'), may hold values from -1.5 to 1.5
- slot_up_matrix: bfloat16 [32, 13, 16, 1024], P('adapter'), may hold values from -0.1875 to 0.1875
- down_matrix_rows: float32 [128, 16, 8192], P('adapter', None, 'tensor'), may hold values from -1.5 to 1.5
- down_first_moment: float32 [128, 16, 8192], P('adapter', None, 'tensor'), may hold values from -12 to 12
- down_second_moment: float32 [128, 16, 8192], P('adapter', None, 'tensor'), may hold values from 1 to 100
- up_matrix_rows: float32 [128, 16, 1024], P('adapter', None, 'tensor'), may hold values from -0.1875 to 0.1875
- up_first_moment: float32 [128, 16, 1024], P('adapter', None, 'tensor'), may hold values from -12 to 12
- up_second_moment: float32 [128, 16, 1024], P('adapter', None, 'tensor'), may hold values from 1 to 100
Outputs:
- in_grad: bfloat16 [65536, 8192], P(('adapter', 'tensor'))
- new_down: float32 [128, 16, 8192], P('adapter', None, 'tensor')
- new_down_m: float32 [128, 16, 8192], P('adapter', None, 'tensor')
- new_down_v: float32 [128, 16, 8192], P('adapter', None, 'tensor')
- new_up: float32 [128, 16, 1024], P('adapter', None, 'tensor')
- new_up_m: float32 [128, 16, 1024], P('adapter', None, 'tensor')
- new_up_v: float32 [128, 16, 1024], P('adapter', None, 'tensor')
The draws below stay inside these ranges and needn't reach their ends.
Inputs may be any that keep to these rules, and one draw needn't show every extreme that they name: `adapter_storage_row`: a permutation. `adapter_per_slot`: the 13 adapters of a group are distinct; of one group's slots at most 2 have adapters whose storage row lies on one device (rows d * 4 to d * 4 + 3), and exactly 2 do for some device in every group. `segment_first_row`: each row of a group starts at 0, rises strictly, holds multiples of 128, and ends at 1920; slot k's segment runs to the next offset or to the group's end. `adapter_per_row`: within slot k's segment of group g the rows carry adapter_per_slot[g, k], followed by 1 to 127 padding rows that carry 128.
All inputs are finite; a program needn't handle non-finite values.
Results may differ from the reference program's by a relative error of at most 0.0054.
Values may be sent and summed in bfloat16 or wider, within the bound.
A program may use at most 128 MiB of HBM per device.

```python
import math
import jax
import jax.numpy as jnp
from jax import lax

MODEL_WIDTH = 8192
KVW = 1024
ADAPTER_RANK = 16
TILE = 128
STEP = 100
ADP_DEV = 4
GROUPS = 32
SLOTS = 13
ROWS_PER_GROUP = 2048
TILES = 16
TOTAL_TOKENS = 65536
ADAPTERS = 128


def layout_plan(key):
    key_map, key_group = jax.random.split(key)
    adapter_storage_row = jax.random.permutation(key_map, ADAPTERS).astype(jnp.int32)
    adapter_of = jnp.argsort(adapter_storage_row).astype(jnp.int32)

    def one_group(group_key):
        keys = jax.random.split(group_key, 6)
        owners = jax.random.permutation(keys[0], GROUPS).astype(jnp.int32)[:SLOTS - 1]
        owners = jnp.concatenate([owners, owners[:1]])
        first = jax.random.randint(keys[1], (SLOTS - 1,), 0, ADP_DEV).astype(jnp.int32)
        last = (first[0] + jax.random.randint(keys[2], (), 1, ADP_DEV).astype(jnp.int32)) % ADP_DEV
        local = jnp.concatenate([first, last[None]])
        order = jax.random.permutation(keys[3], SLOTS).astype(jnp.int32)
        stored = (owners * ADP_DEV + local)[order]
        slots = adapter_of[stored]
        inner = jax.random.permutation(keys[4], TILES - 2).astype(jnp.int32)[:SLOTS - 2] + 1
        cuts = jnp.sort(jnp.concatenate([inner, jnp.full((1,), TILES - 1, jnp.int32)]))
        tile_start = jnp.concatenate([jnp.zeros((1,), jnp.int32), cuts])
        tile_end = jnp.concatenate([cuts, jnp.full((1,), TILES, jnp.int32)])
        offsets = tile_start * TILE
        lengths = (tile_end - tile_start) * TILE
        padding = jax.random.randint(keys[5], (SLOTS,), 1, TILE).astype(jnp.int32)
        valid = lengths - padding
        rows = jnp.arange(ROWS_PER_GROUP, dtype=jnp.int32)
        segment = jnp.sum((offsets[None, :] <= rows[:, None]).astype(jnp.int32), axis=1) - 1
        position = rows - offsets[segment]
        ids = jnp.where(position < valid[segment], slots[segment], ADAPTERS).astype(jnp.int32)
        return (ids, offsets, slots)
    group_keys = jax.random.split(key_group, GROUPS)
    ids, offsets, slots = jax.vmap(one_group)(group_keys)
    return (ids.reshape(-1), offsets, slots, adapter_storage_row)


def draw_adapter_per_row(key, part):
    return layout_plan(key)[0]


def draw_segment_first_row(key, part):
    return layout_plan(key)[1]


def draw_adapter_per_slot(key, part):
    return layout_plan(key)[2]


def draw_adapter_storage_row(key, part):
    return layout_plan(key)[3]


def shard_levels(own_key, shape, pieces, low, high):
    gain, own = 1.0, jax.random.fold_in(own_key, 6)
    for dim, parts in pieces:
        draws = jnp.exp(jax.random.uniform(jax.random.fold_in(own, dim), (parts,), jnp.float32, low / len(pieces), high / len(pieces)))
        gain = gain * jnp.repeat(draws, shape[dim] // parts).reshape([-1 if axis == dim else 1 for axis in range(len(shape))])
    return gain


def noise(own_key, extent, deviation, reach, shards=(), held_as=jnp.bfloat16):
    level = shard_levels(own_key, extent, shards, -0.22, 0.18) if shards else 1.0
    values = jax.random.normal(own_key, extent, jnp.float32) * deviation * level
    return jnp.minimum(jnp.maximum(values, -reach), reach).astype(held_as)


def setup_inputs(seed: int = 0) -> dict:
    key_list = jax.random.split(jax.random.key(seed), 17)
    acts = noise(key_list[0], (TOTAL_TOKENS, MODEL_WIDTH), 1.0, 6.0, ((0, 256),))
    output_gradient = noise(key_list[1], (TOTAL_TOKENS, KVW), 1.0, 6.0, ((0, 256),))
    adapter_middle_saved = noise(key_list[2], (TOTAL_TOKENS, ADAPTER_RANK), 0.5, 4.0, ((0, 256),))
    adapter_per_row = draw_adapter_per_row(jax.random.fold_in(key_list[16], 71), 0)
    segment_first_row = draw_segment_first_row(jax.random.fold_in(key_list[16], 71), 0)
    adapter_per_slot = draw_adapter_per_slot(jax.random.fold_in(key_list[16], 71), 0)
    adapter_storage_row = draw_adapter_storage_row(jax.random.fold_in(key_list[16], 71), 0)
    frozen_value_weight = noise(key_list[7], (MODEL_WIDTH, KVW), KVW ** -0.5, 0.1875, ((0, 8),))
    slot_down_matrix = noise(key_list[8], (GROUPS, SLOTS, ADAPTER_RANK, MODEL_WIDTH), ADAPTER_RANK ** -0.5, 1.5, ((0, 32), (3, 8)))
    slot_up_matrix = noise(key_list[9], (GROUPS, SLOTS, ADAPTER_RANK, KVW), KVW ** -0.5, 0.1875, ((0, 32),))
    down_matrix_rows = noise(key_list[10], (ADAPTERS, ADAPTER_RANK, MODEL_WIDTH), ADAPTER_RANK ** -0.5, 1.5, ((0, 32), (2, 8)), jnp.float32)
    down_first_moment = noise(key_list[11], (ADAPTERS, ADAPTER_RANK, MODEL_WIDTH), 2.0, 12.0, ((0, 32), (2, 8)), jnp.float32)
    down_second_moment = jnp.clip(jnp.exp(math.log(100.0) - 4.6051702 * jax.random.uniform(key_list[12], (ADAPTERS, ADAPTER_RANK, MODEL_WIDTH), jnp.float32) ** shard_levels(key_list[12], (ADAPTERS, ADAPTER_RANK, MODEL_WIDTH), ((0, 32), (2, 8)), -0.2, 0.2)), 1.0, 100.0)
    up_matrix_rows = noise(key_list[13], (ADAPTERS, ADAPTER_RANK, KVW), KVW ** -0.5, 0.1875, ((0, 32), (2, 8)), jnp.float32)
    up_first_moment = noise(key_list[14], (ADAPTERS, ADAPTER_RANK, KVW), 2.0, 12.0, ((0, 32), (2, 8)), jnp.float32)
    up_second_moment = jnp.clip(jnp.exp(math.log(100.0) - 4.6051702 * jax.random.uniform(key_list[15], (ADAPTERS, ADAPTER_RANK, KVW), jnp.float32) ** shard_levels(key_list[15], (ADAPTERS, ADAPTER_RANK, KVW), ((0, 32), (2, 8)), -0.2, 0.2)), 1.0, 100.0)
    return dict(acts=acts, output_gradient=output_gradient, adapter_middle_saved=adapter_middle_saved, adapter_per_row=adapter_per_row, segment_first_row=segment_first_row, adapter_per_slot=adapter_per_slot, adapter_storage_row=adapter_storage_row, frozen_value_weight=frozen_value_weight, slot_down_matrix=slot_down_matrix, slot_up_matrix=slot_up_matrix, down_matrix_rows=down_matrix_rows, down_first_moment=down_first_moment, down_second_moment=down_second_moment, up_matrix_rows=up_matrix_rows, up_first_moment=up_first_moment, up_second_moment=up_second_moment)


adapter_scale = 0.5
beta_one = 0.9
beta_two = 0.999
adam_eps = 1e-08
learn_rate = 0.01

def adam_update(param, first, second, grad):
    first_new = beta_one * first + (1.0 - beta_one) * grad
    second_new = beta_two * second + (1.0 - beta_two) * grad * grad
    bias_one = 1.0 - beta_one ** STEP
    bias_two = 1.0 - beta_two ** STEP
    moved = first_new / bias_one / (jnp.sqrt(second_new / bias_two) + adam_eps)
    return (param - learn_rate * moved, first_new, second_new)

def reference(acts, output_gradient, adapter_middle_saved, adapter_per_row, segment_first_row, adapter_per_slot, adapter_storage_row, frozen_value_weight, slot_down_matrix, slot_up_matrix, down_matrix_rows, down_first_moment, down_second_moment, up_matrix_rows, up_first_moment, up_second_moment):

    def one_group(index):
        start_row = index * ROWS_PER_GROUP
        rows_in = lax.dynamic_slice_in_dim(acts, start_row, ROWS_PER_GROUP, 0)
        rows_grad = lax.dynamic_slice_in_dim(output_gradient, start_row, ROWS_PER_GROUP, 0)
        middle_rows = lax.dynamic_slice_in_dim(adapter_middle_saved, start_row, ROWS_PER_GROUP, 0)
        rows_ids = lax.dynamic_slice_in_dim(adapter_per_row, start_row, ROWS_PER_GROUP, 0)
        offsets = segment_first_row[index]
        slots = adapter_per_slot[index]
        downs = slot_down_matrix[index]
        ups = slot_up_matrix[index]
        group_member = rows_ids[:, None] == slots[None, :]
        projected_rows = jnp.einsum('nc,krc->nkr', rows_grad.astype(jnp.float32), ups.astype(jnp.float32))
        backward_middle = (adapter_scale * lax.optimization_barrier(jnp.sum(jnp.where(group_member[:, :, None], projected_rows, 0.0), axis=1))).astype(jnp.bfloat16)
        retained_middle = jnp.where((rows_ids < ADAPTERS)[:, None], middle_rows, jnp.zeros_like(middle_rows))
        starts = jnp.arange(TILES, dtype=jnp.int32) * TILE
        tile_slot = lax.optimization_barrier(jnp.sum((offsets[None, :] <= starts[:, None]).astype(jnp.int32), axis=1)) - 1
        slot_lookup_table = (tile_slot[None, :] == jnp.arange(SLOTS, dtype=jnp.int32)[:, None]).astype(jnp.float32)
        frozen_share = jnp.dot(rows_grad, frozen_value_weight.T, preferred_element_type=jnp.float32)
        backward_blocks = backward_middle.reshape(TILES, TILE, ADAPTER_RANK).astype(jnp.float32)
        down_blocks = downs[tile_slot].astype(jnp.float32)
        adapter_share = jnp.einsum('ahw,awu->ahu', backward_blocks, down_blocks).reshape(ROWS_PER_GROUP, MODEL_WIDTH)
        input_rows = (frozen_share + adapter_share).astype(jnp.bfloat16)
        down_pieces = jnp.einsum('tkr,tkd->trd', backward_blocks, rows_in.reshape(TILES, TILE, MODEL_WIDTH).astype(jnp.float32))
        down_slot = jnp.einsum('st,trd->srd', slot_lookup_table, down_pieces, precision=lax.Precision.HIGHEST)
        up_fragments = jnp.einsum('tkr,tkc->trc', retained_middle.reshape(TILES, TILE, ADAPTER_RANK).astype(jnp.float32), rows_grad.reshape(TILES, TILE, KVW).astype(jnp.float32))
        slot_up_gradient = adapter_scale * jnp.einsum('qz,zli->qli', slot_lookup_table, up_fragments, precision=lax.Precision.HIGHEST)
        stored = adapter_storage_row[slots]
        return (input_rows, down_slot, slot_up_gradient, stored)
    input_rows, down_slots, up_slots, stored = lax.map(one_group, jnp.arange(GROUPS, dtype=jnp.int32))
    in_grad = input_rows.reshape(TOTAL_TOKENS, MODEL_WIDTH)
    flat_rows = stored.reshape(-1)
    grad_down = jax.ops.segment_sum(down_slots.reshape(-1, ADAPTER_RANK, MODEL_WIDTH), flat_rows, num_segments=ADAPTERS)
    grad_up = jax.ops.segment_sum(up_slots.reshape(-1, ADAPTER_RANK, KVW), flat_rows, num_segments=ADAPTERS)
    new_down, new_down_m, new_down_v = adam_update(down_matrix_rows, down_first_moment, down_second_moment, grad_down)
    new_up, new_up_m, new_up_v = adam_update(up_matrix_rows, up_first_moment, up_second_moment, grad_up)
    return (in_grad, new_down, new_down_m, new_down_v, new_up, new_up_m, new_up_v)
```

```python
import jax
import jax.numpy as jnp
from jax import lax
from jax.experimental import pallas as pl
from jax.experimental.pallas import tpu as pltpu
from jax.sharding import PartitionSpec as P

MESH = pl.DeviceIdType.MESH
TILE = 128
STEP = 100
NX, NY, NZ = 4, 4, 8

adapter_scale = 0.5
beta_one = 0.9
beta_two = 0.999
adam_eps = 1e-08
learn_rate = 0.01

ROWS = 256
WIDTH = 8192
KVW = 1024
RANK = 16
SLOTS = 13
TILES = 16
COLS = 1024
UPC = 128
PAY = COLS + UPC
CHUNK = 128
STORED = 4
A, B, C, X, AX, BX, DX = range(7)
F32 = jnp.float32
BF16 = jnp.bfloat16


def adam_update(param, first, second, grad):
    first_new = beta_one * first + (1.0 - beta_one) * grad
    second_new = beta_two * second + (1.0 - beta_two) * grad * grad
    bias_one = 1.0 - beta_one**STEP
    bias_two = 1.0 - beta_two**STEP
    moved = first_new / bias_one / (jnp.sqrt(second_new / bias_two) + adam_eps)
    return (param - learn_rate * moved, first_new, second_new)


def kernel(
    acts_h, og_h, mid, rid, seg, aps, stor, w_h, sd_h, su_h,
    out_h, gd, gu,
    acts, og, sd, su, w, xd, dn, gs, gr, sl, dns, us, ur, ds, dr, bmt, ost,
    tslot, sr, tab,
    in_sem, out_sem, w_send, w_recv, sib_recv, dn_send, dn_recv, g_send, g_recv,
    s_send, s_recv, r_send, r_recv, loc_sem,
):
    a = lax.axis_index("adapter")
    t = lax.axis_index("tensor")
    z, xh, c = a // 4, (a // 2) % 2, a % 2
    y, xl = t // 2, t % 2
    x = xh * 2 + xl

    def dev(dx=0, dy=0, dz=0, dc=0):
        x_, y_, z_, c_ = (x + dx) % NX, (y + dy) % NY, (z + dz) % NZ, (c + dc) % 2
        return (z_ * 4 + (x_ // 2) * 2 + c_, y_ * 2 + x_ % 2)

    def peer(dy, dx):
        return (a, ((y + dy) % NY) * 2 + (xl + dx) % 2)

    loads = {}
    for i, (name, src, dst) in enumerate(
        (
            ("og", og_h, og),
            ("su", su_h, su),
            ("sd", sd_h, sd),
            ("acts", acts_h, acts),
            ("w", w_h, w.at[t]),
        )
    ):
        loads[name] = pltpu.make_async_copy(src, dst, in_sem.at[i])
        loads[name].start()

    barrier = pltpu.get_barrier_semaphore()
    friends = [peer(dy, dx) for dy in range(4) for dx in range(2) if (dy, dx) != (0, 0)]
    other = 1 - 2 * (1 - xl)
    friends += [dev(dx=other), dev(dx=2), dev(dz=1), dev(dz=-1), dev(dc=1)]
    for f in friends:
        pl.semaphore_signal(barrier, inc=1, device_id=f, device_id_type=MESH)

    def tile_slot(j, _):
        n = jnp.int32(-1)
        for k in range(SLOTS):
            n = n + (seg[0, k] <= j * TILE).astype(jnp.int32)
        tslot[j] = n
        return 0

    lax.fori_loop(0, TILES, tile_slot, 0)

    loads["og"].wait()
    loads["su"].wait()
    kept = []
    for i in range(2):
        slot = tslot[2 * t + i]
        ids = rid[:, i * TILE : (i + 1) * TILE]
        prod = lax.dot_general(
            su[slot], og[i * TILE : (i + 1) * TILE], (((1,), (1,)), ((), ())), preferred_element_type=F32
        )
        bmt[i] = jnp.where(ids == aps[a, slot], adapter_scale * prod, 0.0).astype(BF16)
        m = mid[i * TILE : (i + 1) * TILE].astype(F32).T
        kept.append(jnp.where(ids < stor.shape[0], m, 0.0).astype(BF16))

    pl.semaphore_wait(barrier, len(friends))

    e = z % 2
    p0, p1 = 2 * e, 2 * e + 1
    n0, n1 = 2 * (1 - e), 2 * (1 - e) + 1
    where = {
        A: ((y + 1) % 4) * 2 + xl,
        B: ((y + 3) % 4) * 2 + xl,
        C: ((y + 2) % 4) * 2 + xl,
        X: y * 2 + 1 - xl,
        AX: ((y + 1) % 4) * 2 + 1 - xl,
        BX: ((y + 3) % 4) * 2 + 1 - xl,
        DX: ((y + 2) % 4) * 2 + 1 - xl,
    }
    sent = []

    def region(piece, chunk, half):
        return w.at[piece, pl.ds(pl.multiple_of(half * 512 + chunk * CHUNK, CHUNK), CHUNK)]

    def push(src, dst, sem, target):
        cp = pltpu.make_async_remote_copy(
            src_ref=src, dst_ref=dst, send_sem=w_send.at[len(sent)], recv_sem=sem, device_id=target, device_id_type=MESH
        )
        cp.start()
        sent.append(cp)

    def push_own(chunk, label, target):
        src = w_h.at[pl.ds(pl.multiple_of(c * 512 + chunk * CHUNK, CHUNK), CHUNK)]
        push(src, region(t, chunk, c), w_recv.at[label, chunk], target)

    def pass_on(label, chunk, new, target):
        place = region(where[label], chunk, c)
        push(place, place, w_recv.at[new, chunk], target)

    def arrived(label, chunk):
        place = region(where[label], chunk, c)
        pltpu.make_async_copy(place, place, w_recv.at[label, chunk]).wait()
        push(place, place, sib_recv.at[label, chunk], dev(dc=1))

    def sib_arrived(label):
        for chunk in range(4):
            place = region(where[label], chunk, 1 - c)
            pltpu.make_async_copy(place, place, sib_recv.at[label, chunk]).wait()

    up_y, dn_y, up_x, dn_x, up_z, dn_z = dev(dy=1), dev(dy=-1), dev(dx=1), dev(dx=-1), dev(dz=1), dev(dz=-1)

    push_own(p0, B, up_y)
    push_own(p0, A, dn_y)
    push_own(p0, X, up_x)
    push_own(p1, X, dn_x)
    push_own(p1, B, up_y)
    push_own(p1, A, dn_y)

    loads["acts"].wait()
    for i in range(2):
        upg = adapter_scale * jnp.dot(kept[i], og[i * TILE : (i + 1) * TILE], preferred_element_type=F32)
        upg = upg.astype(BF16)
        for u in range(8):
            gs[u, i, :, COLS:] = upg[:, u * UPC : (u + 1) * UPC]
    order = [(2, 1), (2, 0), (1, 1), (3, 1), (0, 1), (1, 0), (3, 0), (0, 0)]
    g_sent = []
    for n, (dy, dx) in enumerate(order):
        u = ((y + dy) % 4) * 2 + (xl + dx) % 2
        for i in range(2):
            block = acts[i * TILE : (i + 1) * TILE, pl.ds(pl.multiple_of(u * COLS, COLS), COLS)]
            gs[u, i, :, :COLS] = jnp.dot(bmt[i], block, preferred_element_type=F32).astype(BF16)
        if (dy, dx) == (0, 0):
            gr[t] = gs[t]
        else:
            cp = pltpu.make_async_remote_copy(
                src_ref=gs.at[u], dst_ref=gr.at[t], send_sem=g_send.at[n], recv_sem=g_recv.at[n],
                device_id=peer(dy, dx), device_id_type=MESH,
            )
            cp.start()
            g_sent.append(cp)

    loads["sd"].wait()

    def spread(j, _):
        xd[j] = sd[tslot[j]]
        return 0

    lax.fori_loop(0, TILES, spread, 0)
    dn_sent = []
    for n, (dy, dx) in enumerate(order):
        u = ((y + dy) % 4) * 2 + (xl + dx) % 2
        if (dy, dx) == (0, 0):
            dn[t] = xd[pl.ds(2 * t, 2)]
        else:
            cp = pltpu.make_async_remote_copy(
                src_ref=xd.at[pl.ds(2 * u, 2)], dst_ref=dn.at[t], send_sem=dn_send.at[n], recv_sem=dn_recv.at[n],
                device_id=peer(dy, dx), device_id_type=MESH,
            )
            cp.start()
            dn_sent.append(cp)

    def in_grad(piece, n):
        def block(j, _):
            rows = pl.ds(pl.multiple_of(j * 256, 256), 256)
            cols = pl.ds(pl.multiple_of(piece * COLS + j * 256, 256), 256)
            full = lax.dot_general(og[...], w[piece, rows], (((1,), (1,)), ((), ())), preferred_element_type=F32)
            for i in range(2):
                low = lax.dot_general(
                    bmt[i], dn[piece, i, :, rows], (((0,), (0,)), ((), ())), preferred_element_type=F32
                )
                ost[i * TILE : (i + 1) * TILE, cols] = (full[i * TILE : (i + 1) * TILE] + low).astype(BF16)
            return 0

        lax.fori_loop(0, 4, block, 0)
        cols = pl.ds(pl.multiple_of(piece * COLS, COLS), COLS)
        cp = pltpu.make_async_copy(ost.at[:, cols], out_h.at[:, cols], out_sem.at[n])
        cp.start()
        return cp

    arrived(A, p0)
    pass_on(A, p0, AX, up_x)
    pass_on(A, p0, C, dn_y)
    arrived(B, p0)
    pass_on(B, p0, BX, dn_x)
    arrived(X, p0)
    pass_on(X, p0, X, up_z)
    arrived(X, p1)
    pass_on(X, p1, X, dn_z)
    arrived(A, p1)
    pass_on(A, p1, AX, dn_x)
    arrived(B, p1)
    pass_on(B, p1, BX, up_x)
    pass_on(B, p1, C, up_y)
    push_own(n0, B, up_y)
    push_own(n0, A, dn_y)
    push_own(n1, B, up_y)
    push_own(n1, A, dn_y)

    outs = []
    loads["w"].wait()
    outs.append(in_grad(t, 0))

    for q in range(4):
        group = z * 4 + (xh ^ (q % 2)) * 2 + (c ^ (q // 2))
        for k in range(SLOTS):
            sr[q * SLOTS + k] = stor[aps[group, k]]

    def find(n, _):
        q, rest = n // 32, n % 32
        row = ((z + rest // 4) % NZ) * 16 + xh * 8 + c * 4 + rest % 4
        k_found = jnp.int32(0)
        for k in range(SLOTS):
            k_found = jnp.where(sr[q * SLOTS + k] == row, k + 1, k_found)
        tab[n] = k_found
        return 0

    lax.fori_loop(0, 128, find, 0)

    for n, (dy, dx) in enumerate(order[:-1]):
        src = ((y + dy) % 4) * 2 + (xl + dx) % 2
        back = order.index(((4 - dy) % 4, dx))
        pltpu.make_async_copy(gr.at[src], gr.at[src], g_recv.at[back]).wait()
    for k in range(SLOTS):
        first = seg[0, k] // TILE
        last = seg[0, k + 1] // TILE if k + 1 < SLOTS else TILES
        total = jnp.zeros((RANK, PAY), F32)
        for i in range(4):
            j = jnp.minimum(first + i, TILES - 1)
            total = total + jnp.where(first + i < last, gr[j // 2, j % 2].astype(F32), 0.0)
        sl[0, k] = total.astype(BF16)
    s_sent = []

    def send_slots(n, src, dst, target):
        cp = pltpu.make_async_remote_copy(
            src_ref=sl.at[src], dst_ref=sl.at[dst], send_sem=s_send.at[n], recv_sem=s_recv.at[dst - 1],
            device_id=target, device_id_type=MESH,
        )
        cp.start()
        s_sent.append(cp)

    send_slots(0, 0, 1, dev(dx=2))
    send_slots(1, 0, 2, dev(dc=1))

    arrived(AX, p0)
    pass_on(AX, p0, AX, up_z)
    arrived(BX, p0)
    pass_on(BX, p0, BX, dn_z)
    arrived(C, p0)
    pass_on(C, p0, DX, up_x)
    arrived(C, p1)
    pass_on(C, p1, DX, dn_x)
    arrived(AX, p1)
    pass_on(AX, p1, AX, dn_z)
    arrived(BX, p1)
    pass_on(BX, p1, BX, up_z)
    pass_on(C, p0, C, up_z)
    pass_on(C, p1, C, dn_z)

    pltpu.make_async_copy(sl.at[1], sl.at[1], s_recv.at[0]).wait()
    send_slots(2, 1, 3, dev(dc=1))
    pltpu.make_async_copy(sl.at[2], sl.at[2], s_recv.at[1]).wait()
    pltpu.make_async_copy(sl.at[3], sl.at[3], s_recv.at[2]).wait()

    def gather_rows(dz):
        def one(r, _):
            total = jnp.zeros((RANK, PAY), F32)
            for q in range(4):
                k = tab[q * 32 + dz * 4 + r]
                total = total + jnp.where(k > 0, sl[q, jnp.maximum(k - 1, 0)].astype(F32), 0.0)
            dns[dz, r] = total
            return 0

        lax.fori_loop(0, STORED, one, 0)

    r_sent = []

    def ring_send(src, dst, direction, step, target):
        n = direction * 4 + step
        cp = pltpu.make_async_remote_copy(
            src_ref=src, dst_ref=dst, send_sem=r_send.at[n], recv_sem=r_recv.at[n], device_id=target, device_id_type=MESH
        )
        cp.start()
        r_sent.append(cp)

    def ring_wait(ref, direction, step):
        pltpu.make_async_copy(ref, ref, r_recv.at[direction * 4 + step]).wait()

    gather_rows(4)
    us[0, 0:2] = dns[4, 0:2].astype(BF16)
    ds[0, 2:4] = dns[4, 2:4].astype(BF16)
    ring_send(us.at[0, pl.ds(0, 2)], ur.at[0, pl.ds(0, 2)], 0, 0, up_z)
    ring_send(ds.at[0, pl.ds(2, 2)], dr.at[0, pl.ds(2, 2)], 1, 0, dn_z)
    gather_rows(3)
    gather_rows(5)
    ring_wait(ur.at[0, pl.ds(0, 2)], 0, 0)
    us[1, 0:2] = (dns[3, 0:2] + ur[0, 0:2].astype(F32)).astype(BF16)
    us[1, 2:4] = dns[3, 2:4].astype(BF16)
    ring_send(us.at[1], ur.at[1], 0, 1, up_z)
    ring_wait(dr.at[0, pl.ds(2, 2)], 1, 0)
    ds[1, 0:2] = dns[5, 0:2].astype(BF16)
    ds[1, 2:4] = (dns[5, 2:4] + dr[0, 2:4].astype(F32)).astype(BF16)
    ring_send(ds.at[1], dr.at[1], 1, 1, dn_z)
    for dz in (2, 6, 1, 7, 0):
        gather_rows(dz)
    arrived(DX, p0)
    pass_on(DX, p0, DX, up_z)
    arrived(DX, p1)
    pass_on(DX, p1, DX, dn_z)
    for step in (2, 3):
        ring_wait(ur.at[step - 1], 0, step - 1)
        us[step] = (dns[4 - step] + ur[step - 1].astype(F32)).astype(BF16)
        ring_send(us.at[step], ur.at[step], 0, step, up_z)
        ring_wait(dr.at[step - 1], 1, step - 1)
        ds[step] = (dns[4 + step] + dr[step - 1].astype(F32)).astype(BF16)
        ring_send(ds.at[step], dr.at[step], 1, step, dn_z)
        if step == 2:
            for n, (dy, dx) in enumerate(order[:-1]):
                src = ((y + dy) % 4) * 2 + (xl + dx) % 2
                back = order.index(((4 - dy) % 4, dx))
                pltpu.make_async_copy(dn.at[src], dn.at[src], dn_recv.at[back]).wait()
            for label in (A, B):
                arrived(label, n0)
                arrived(label, n1)
            for label in (X, AX, BX):
                arrived(label, n0)
                arrived(label, n1)
            for n, label in enumerate((A, B)):
                sib_arrived(label)
                outs.append(in_grad(where[label], 1 + n))
    arrived(C, n0)
    arrived(C, n1)
    arrived(DX, n0)
    arrived(DX, n1)
    for n, label in enumerate((X, AX, BX)):
        sib_arrived(label)
        outs.append(in_grad(where[label], 3 + n))
    ring_wait(ur.at[3], 0, 3)
    ring_wait(dr.at[3], 1, 3)
    total = dns[0] + ur[3].astype(F32) + dr[3].astype(F32)
    gd[...] = total[:, :, :COLS]
    gu[...] = total[:, :, COLS:]
    for n, label in enumerate((C, DX)):
        sib_arrived(label)
        outs.append(in_grad(where[label], 6 + n))

    for cp in sent + g_sent + dn_sent + s_sent + r_sent:
        cp.wait_send()
    for cp in outs:
        cp.wait()


def body(
    acts, output_gradient, adapter_middle_saved, adapter_per_row, segment_first_row, adapter_per_slot,
    adapter_storage_row, frozen_value_weight, slot_down_matrix, slot_up_matrix, down_matrix_rows,
    down_first_moment, down_second_moment, up_matrix_rows, up_first_moment, up_second_moment,
):
    vmem = pl.BlockSpec(memory_space=pltpu.VMEM)
    smem = pl.BlockSpec(memory_space=pltpu.SMEM)
    hbm = pl.BlockSpec(memory_space=pl.ANY)
    dma = pltpu.SemaphoreType.DMA
    in_grad, grad_down, grad_up = pl.pallas_call(
        kernel,
        out_shape=(
            jax.ShapeDtypeStruct((ROWS, WIDTH), BF16),
            jax.ShapeDtypeStruct((STORED, RANK, COLS), F32),
            jax.ShapeDtypeStruct((STORED, RANK, UPC), F32),
        ),
        in_specs=[hbm, hbm, vmem, vmem, smem, smem, smem, hbm, hbm, hbm],
        out_specs=(hbm, vmem, vmem),
        scratch_shapes=[
            pltpu.VMEM((ROWS, WIDTH), BF16),
            pltpu.VMEM((ROWS, KVW), BF16),
            pltpu.VMEM((SLOTS, RANK, COLS), BF16),
            pltpu.VMEM((SLOTS, RANK, KVW), BF16),
            pltpu.VMEM((8, COLS, KVW), BF16),
            pltpu.VMEM((TILES, RANK, COLS), BF16),
            pltpu.VMEM((8, 2, RANK, COLS), BF16),
            pltpu.VMEM((8, 2, RANK, PAY), BF16),
            pltpu.VMEM((8, 2, RANK, PAY), BF16),
            pltpu.VMEM((4, SLOTS, RANK, PAY), BF16),
            pltpu.VMEM((NZ, STORED, RANK, PAY), F32),
            pltpu.VMEM((4, STORED, RANK, PAY), BF16),
            pltpu.VMEM((4, STORED, RANK, PAY), BF16),
            pltpu.VMEM((4, STORED, RANK, PAY), BF16),
            pltpu.VMEM((4, STORED, RANK, PAY), BF16),
            pltpu.VMEM((2, RANK, TILE), BF16),
            pltpu.VMEM((ROWS, WIDTH), BF16),
            pltpu.SMEM((TILES,), jnp.int32),
            pltpu.SMEM((4 * SLOTS,), jnp.int32),
            pltpu.SMEM((128,), jnp.int32),
            dma((5,)),
            dma((8,)),
            dma((64,)),
            dma((7, 4)),
            dma((7, 4)),
            dma((7,)),
            dma((7,)),
            dma((7,)),
            dma((7,)),
            dma((3,)),
            dma((3,)),
            dma((8,)),
            dma((8,)),
            dma((1,)),
        ],
        compiler_params=pltpu.CompilerParams(collective_id=0, has_side_effects=True, vmem_limit_bytes=56 << 20),
        cost_estimate=pl.CostEstimate(flops=2 * ROWS * WIDTH * KVW, bytes_accessed=12 << 20, transcendentals=0),
        name="fused",
    )(
        acts, output_gradient, adapter_middle_saved, adapter_per_row.reshape(1, ROWS), segment_first_row,
        adapter_per_slot, adapter_storage_row, frozen_value_weight, slot_down_matrix[0], slot_up_matrix[0],
    )
    new_down, new_down_m, new_down_v = adam_update(down_matrix_rows, down_first_moment, down_second_moment, grad_down)
    new_up, new_up_m, new_up_v = adam_update(up_matrix_rows, up_first_moment, up_second_moment, grad_up)
    return (in_grad, new_down, new_down_m, new_down_v, new_up, new_up_m, new_up_v)


def solution(mesh):
    rows = ("adapter", "tensor")
    stored = P("adapter", None, "tensor")
    in_specs = (
        P(rows, None), P(rows, None), P(rows, None), P(rows), P("adapter", None), P(), P(), P("tensor", None),
        P("adapter", None, None, "tensor"), P("adapter", None, None, None),
        stored, stored, stored, stored, stored, stored,
    )
    out_specs = (P(rows, None),) + (stored,) * 6
    return jax.shard_map(body, mesh=mesh, in_specs=in_specs, out_specs=out_specs, check_vma=False)
```

```python
import jax
import jax.numpy as jnp
from jax import lax
from jax.experimental import pallas as pl
from jax.experimental.pallas import tpu as pltpu
from jax.sharding import PartitionSpec as P

MESH = pl.DeviceIdType.MESH
TILE = 128
STEP = 100
NX, NY, NZ = 4, 4, 8

adapter_scale = 0.5
beta_one = 0.9
beta_two = 0.999
adam_eps = 1e-08
learn_rate = 0.01

ROWS = 256
WIDTH = 8192
KVW = 1024
RANK = 16
SLOTS = 13
TILES = 16
COLS = 1024
UPC = 128
PAY = COLS + UPC
CHUNK = 128
STORED = 4
A, B, C, X, AX, BX, DX = range(7)
CUTS = ((0, 640), (640, PAY))
BLOCK = 256
VMEM_LIMIT = 56 << 20
SEQ = (
    ("own_y", 0), ("own_x",), ("own_y", 1),
    ("tiles", 0), ("tiles", 1),
    ("in", A, 0), ("in", B, 0), ("in", X, 0), ("in", X, 1), ("in", A, 1), ("in", B, 1),
    ("tables",), ("slots", 0), ("slots", 1),
    ("in", A, 2), ("in", B, 3), ("in", AX, 0), ("in", BX, 0), ("in", C, 0),
    ("ring", 0, 0), ("ring", 0, 1), ("rest", 0), ("rest", 1),
    ("in", AX, 1), ("in", BX, 1), ("in", C, 1),
    ("ring", 1, 0), ("ring", 1, 1),
    ("downs",),
    ("ring", 2, 0), ("ring", 2, 1),
    ("in", AX, 2), ("in", BX, 3),
    ("ring", 3, 0), ("ring", 3, 1),
    ("cols", None),
    ("in", A, 3), ("in", B, 2), ("in", X, 2), ("in", X, 3),
    ("ring", 4, 0), ("ring", 4, 1),
    ("in", AX, 3), ("in", BX, 2),
    ("in", C, 2), ("in", C, 3), ("in", DX, 0), ("in", DX, 1),
    ("wait_down",), ("cols", A), ("cols", B), ("cols", X), ("cols", AX), ("cols", BX), ("cols", C),
    ("in", DX, 2), ("in", DX, 3), ("cols", DX),
)
F32 = jnp.float32
BF16 = jnp.bfloat16


def adam_update(param, first, second, grad):
    first_new = beta_one * first + (1.0 - beta_one) * grad
    second_new = beta_two * second + (1.0 - beta_two) * grad * grad
    bias_one = 1.0 - beta_one**STEP
    bias_two = 1.0 - beta_two**STEP
    moved = first_new / bias_one / (jnp.sqrt(second_new / bias_two) + adam_eps)
    return (param - learn_rate * moved, first_new, second_new)


def kernel(
    acts_h, og_h, midt, rid, seg, apst, stor, w_h, sd_h, su_h,
    out_h, gd, gu,
    acts, og, sd, su, w, xd, dn,
    gs0, gs1, gr0, gr1, sl0, sl1, dns0, dns1, us0, us1, ur0, ur1, ds0, ds1, dr0, dr1,
    bmt, bm2, ost, tslot, seg2, sr, tab,
    in_sem, out_sem, w_send, w_recv, sib_recv, dn_send, dn_recv, g_send, g_recv,
    s_send, s_recv, r_send, r_recv, m_sem,
):
    gs, gr, sl, dns = (gs0, gs1), (gr0, gr1), (sl0, sl1), (dns0, dns1)
    us, ur, ds, dr = (us0, us1), (ur0, ur1), (ds0, ds1), (dr0, dr1)
    parts = range(len(CUTS))
    a = lax.axis_index("adapter")
    t = lax.axis_index("tensor")
    z, xh, c = a // 4, (a // 2) % 2, a % 2
    y, xl = t // 2, t % 2
    x = xh * 2 + xl

    def dev(dx=0, dy=0, dz=0, dc=0):
        x_, y_, z_, c_ = (x + dx) % NX, (y + dy) % NY, (z + dz) % NZ, (c + dc) % 2
        return (z_ * 4 + (x_ // 2) * 2 + c_, y_ * 2 + x_ % 2)

    def peer(dy, dx, flip=0):
        return (z * 4 + ((xh + flip) % 2) * 2 + c, ((y + dy) % NY) * 2 + (xl + dx) % 2)

    def tensor_of(dy, dx):
        return ((y + dy) % 4) * 2 + (xl + dx) % 2

    loads = {}
    for i, (name, src, dst) in enumerate(
        (
            ("og", og_h, og),
            ("su", su_h, su),
            ("acts", acts_h, acts),
            ("sd", sd_h, sd),
            ("w", w_h, w.at[t]),
        )
    ):
        loads[name] = pltpu.make_async_copy(src, dst, in_sem.at[i])
        loads[name].start()

    plane = [(2, 1), (2, 0), (1, 1), (3, 1), (0, 1), (1, 0), (3, 0), (0, 0)]
    order = [(dy, dx, flip) for dy, dx in plane for flip in (1, 0)]
    barrier = pltpu.get_barrier_semaphore()
    friends = [peer(*d) for d in order[:-1]] + [dev(dz=1), dev(dz=-1), dev(dc=1)]
    for f in friends:
        pl.semaphore_signal(barrier, inc=1, device_id=f, device_id_type=MESH)

    def tile_slot(j, _):
        n = jnp.int32(-1)
        for k in range(SLOTS):
            n = n + (seg[0, k] <= j * TILE).astype(jnp.int32)
        tslot[j] = n
        return 0

    lax.fori_loop(0, TILES, tile_slot, 0)

    loads["og"].wait()
    loads["su"].wait()
    kept = []
    bmt[...] = jnp.zeros_like(bmt)
    for i in range(2):
        slot = tslot[2 * t + i]
        ids = rid[:, i * TILE : (i + 1) * TILE]
        prod = lax.dot_general(
            su[slot], og[i * TILE : (i + 1) * TILE], (((1,), (1,)), ((), ())), preferred_element_type=F32
        )
        own = jnp.where(ids == apst[slot, a], adapter_scale * prod, 0.0)
        bmt[i * RANK : (i + 1) * RANK, i * TILE : (i + 1) * TILE] = own.astype(BF16)
        m = midt[:, i * TILE : (i + 1) * TILE]
        kept.append(jnp.where(ids < stor.shape[0], m, jnp.zeros_like(m)))
    bm2[...] = bmt[...].astype(F32).T.astype(BF16)

    pl.semaphore_wait(barrier, len(friends))

    seg_copy = pltpu.make_async_remote_copy(
        src_ref=seg, dst_ref=seg2, send_sem=m_sem.at[0], recv_sem=m_sem.at[1],
        device_id=peer(0, 0, 1), device_id_type=MESH,
    )
    seg_copy.start()

    e = z % 2
    chunks = (2 * e, 2 * e + 1, 2 * (1 - e), 2 * (1 - e) + 1)
    where = {
        A: tensor_of(1, 0), B: tensor_of(3, 0), C: tensor_of(2, 0), X: tensor_of(0, 1),
        AX: tensor_of(1, 1), BX: tensor_of(3, 1), DX: tensor_of(2, 1),
    }
    sent = []

    def region(piece, chunk, half):
        return w.at[piece, pl.ds(pl.multiple_of(half * 512 + chunk * CHUNK, CHUNK), CHUNK)]

    def push(src, dst, sem, target):
        cp = pltpu.make_async_remote_copy(
            src_ref=src, dst_ref=dst, send_sem=w_send.at[len(sent)], recv_sem=sem, device_id=target, device_id_type=MESH
        )
        cp.start()
        sent.append(cp)

    def push_own(chunk, label, target):
        src = w_h.at[pl.ds(pl.multiple_of(c * 512 + chunk * CHUNK, CHUNK), CHUNK)]
        push(src, region(t, chunk, c), w_recv.at[label, chunk], target)

    def sib_arrived(label):
        for chunk in range(4):
            place = region(where[label], chunk, 1 - c)
            pltpu.make_async_copy(place, place, sib_recv.at[label, chunk]).wait()

    up_y, dn_y, up_x, dn_x, up_z, dn_z = dev(dy=1), dev(dy=-1), dev(dx=1), dev(dx=-1), dev(dz=1), dev(dz=-1)

    def own_y(chunk):
        push_own(chunk, B, up_y)
        push_own(chunk, A, dn_y)

    def own_x():
        push_own(chunks[0], X, up_x)
        push_own(chunks[1], X, dn_x)

    g_sent = []

    def tiles_out(p):
        lo, hi = CUTS[p]
        down = min(hi, COLS) - lo
        if p == 0:
            loads["acts"].wait()
        if hi > COLS:
            for i in range(2):
                g = jnp.dot(kept[i], og[i * TILE : (i + 1) * TILE], preferred_element_type=F32)
                g = (adapter_scale * g).astype(BF16)
                for u in range(8):
                    gs[p][u, i, :, down:] = g[:, u * UPC : (u + 1) * UPC]
        for n, (dy, dx, flip) in enumerate(order):
            u = tensor_of(dy, dx)
            if n % 2 == 0:
                for i in range(2):
                    block = acts[i * TILE : (i + 1) * TILE, pl.ds(pl.multiple_of(u * COLS + lo, 128), down)]
                    low = bmt[i * RANK : (i + 1) * RANK, i * TILE : (i + 1) * TILE]
                    gs[p][u, i, :, :down] = jnp.dot(low, block, preferred_element_type=F32).astype(BF16)
            if n == len(order) - 1:
                gr[p][0, t] = gs[p][t]
            else:
                cp = pltpu.make_async_remote_copy(
                    src_ref=gs[p].at[u], dst_ref=gr[p].at[flip, t], send_sem=g_send.at[p, n], recv_sem=g_recv.at[p, n],
                    device_id=peer(dy, dx, flip), device_id_type=MESH,
                )
                cp.start()
                g_sent.append(cp)

    def wait_tiles(p):
        for dy, dx, flip in order[:-1]:
            back = order.index(((4 - dy) % 4, dx, flip))
            place = gr[p].at[flip, tensor_of(dy, dx)]
            pltpu.make_async_copy(place, place, g_recv.at[p, back]).wait()

    dn_sent = []

    def spread(j, _):
        xd[j // 2, pl.ds(pl.multiple_of((j % 2) * RANK, RANK), RANK)] = sd[tslot[j]]
        return 0

    def downs_out():
        loads["sd"].wait()
        lax.fori_loop(0, TILES, spread, 0)
        for n, (dy, dx) in enumerate(plane):
            u = tensor_of(dy, dx)
            if (dy, dx) == (0, 0):
                dn[t] = xd[t]
            else:
                cp = pltpu.make_async_remote_copy(
                    src_ref=xd.at[u], dst_ref=dn.at[t], send_sem=dn_send.at[n], recv_sem=dn_recv.at[n],
                    device_id=peer(dy, dx), device_id_type=MESH,
                )
                cp.start()
                dn_sent.append(cp)

    def wait_down():
        for dy, dx in plane[:-1]:
            place = dn.at[tensor_of(dy, dx)]
            pltpu.make_async_copy(place, place, dn_recv.at[plane.index(((4 - dy) % 4, dx))]).wait()

    outs = []

    def in_grad(piece):
        for j in range(COLS // BLOCK):
            rows = pl.ds(j * BLOCK, BLOCK)
            cols = pl.ds(pl.multiple_of(piece * COLS + j * BLOCK, BLOCK), BLOCK)
            full = lax.dot_general(og[...], w[piece, rows], (((1,), (1,)), ((), ())), preferred_element_type=F32)
            low = jnp.dot(bm2[...], dn[piece, :, rows], preferred_element_type=F32)
            ost[:, cols] = (full + low).astype(BF16)
        cols = pl.ds(pl.multiple_of(piece * COLS, COLS), COLS)
        cp = pltpu.make_async_copy(ost.at[:, cols], out_h.at[:, cols], out_sem.at[len(outs)])
        cp.start()
        outs.append(cp)

    def find(n, _):
        q, rest = n // 32, n % 32
        row = ((z + rest // 4) % NZ) * 16 + xh * 8 + c * 4 + rest % 4
        k_found = jnp.int32(0)
        for k in range(SLOTS):
            k_found = jnp.where(sr[q * SLOTS + k] == row, k + 1, k_found)
        tab[n] = k_found
        return 0

    def tables():
        for q in range(4):
            group = z * 4 + (xh ^ (q % 2)) * 2 + (c ^ (q // 2))
            for k in range(SLOTS):
                sr[q * SLOTS + k] = stor[apst[k, group]]
        lax.fori_loop(0, 128, find, 0)

    s_sent = []

    def slots_out(p):
        if p == 0:
            seg_copy.wait()
        wait_tiles(p)
        for q, table in ((0, seg), (1, seg2)):
            for k in range(SLOTS):
                first = table[0, k] // TILE
                last = table[0, k + 1] // TILE if k + 1 < SLOTS else TILES
                total = jnp.zeros((RANK, sl[p].shape[-1]), F32)
                for i in range(4):
                    j = jnp.minimum(first + i, TILES - 1)
                    total = total + jnp.where(first + i < last, gr[p][q, j // 2, j % 2].astype(F32), 0.0)
                sl[p][q, k] = total.astype(BF16)
        cp = pltpu.make_async_remote_copy(
            src_ref=sl[p].at[pl.ds(0, 2)], dst_ref=sl[p].at[pl.ds(2, 2)], send_sem=s_send.at[p], recv_sem=s_recv.at[p],
            device_id=dev(dc=1), device_id_type=MESH,
        )
        cp.start()
        s_sent.append(cp)

    def gather_rows(p, dz):
        def one(r, _):
            total = jnp.zeros((RANK, sl[p].shape[-1]), F32)
            for q in range(4):
                k = tab[q * 32 + dz * 4 + r]
                total = total + jnp.where(k > 0, sl[p][q, jnp.maximum(k - 1, 0)].astype(F32), 0.0)
            dns[p][dz, r] = total
            return 0

        lax.fori_loop(0, STORED, one, 0)

    r_sent = []

    def ring_send(src, dst, p, direction, step):
        n = direction * 4 + step
        cp = pltpu.make_async_remote_copy(
            src_ref=src, dst_ref=dst, send_sem=r_send.at[p, n], recv_sem=r_recv.at[p, n],
            device_id=dn_z if direction else up_z, device_id_type=MESH,
        )
        cp.start()
        r_sent.append(cp)

    def ring_wait(ref, p, direction, step):
        pltpu.make_async_copy(ref, ref, r_recv.at[p, direction * 4 + step]).wait()

    def ring(step, p):
        if step == 0:
            place = sl[p].at[pl.ds(2, 2)]
            pltpu.make_async_copy(place, place, s_recv.at[p]).wait()
            gather_rows(p, 4)
            us[p][0, 0:2] = dns[p][4, 0:2].astype(BF16)
            ring_send(us[p].at[0, pl.ds(0, 2)], ur[p].at[0, pl.ds(0, 2)], p, 0, 0)
            ds[p][0, 2:4] = dns[p][4, 2:4].astype(BF16)
            ring_send(ds[p].at[0, pl.ds(2, 2)], dr[p].at[0, pl.ds(2, 2)], p, 1, 0)
            gather_rows(p, 3)
            gather_rows(p, 5)
        elif step == 1:
            ring_wait(ur[p].at[0, pl.ds(0, 2)], p, 0, 0)
            us[p][1, 0:2] = (dns[p][3, 0:2] + ur[p][0, 0:2].astype(F32)).astype(BF16)
            us[p][1, 2:4] = dns[p][3, 2:4].astype(BF16)
            ring_send(us[p].at[1], ur[p].at[1], p, 0, 1)
            ring_wait(dr[p].at[0, pl.ds(2, 2)], p, 1, 0)
            ds[p][1, 0:2] = dns[p][5, 0:2].astype(BF16)
            ds[p][1, 2:4] = (dns[p][5, 2:4] + dr[p][0, 2:4].astype(F32)).astype(BF16)
            ring_send(ds[p].at[1], dr[p].at[1], p, 1, 1)
        elif step < 4:
            ring_wait(ur[p].at[step - 1], p, 0, step - 1)
            us[p][step] = (dns[p][4 - step] + ur[p][step - 1].astype(F32)).astype(BF16)
            ring_send(us[p].at[step], ur[p].at[step], p, 0, step)
            ring_wait(dr[p].at[step - 1], p, 1, step - 1)
            ds[p][step] = (dns[p][4 + step] + dr[p][step - 1].astype(F32)).astype(BF16)
            ring_send(ds[p].at[step], dr[p].at[step], p, 1, step)
        else:
            ring_wait(ur[p].at[3], p, 0, 3)
            ring_wait(dr[p].at[3], p, 1, 3)
            total = dns[p][0] + ur[p][3].astype(F32) + dr[p][3].astype(F32)
            lo, hi = CUTS[p]
            down = min(hi, COLS) - lo
            gd[:, :, lo : lo + down] = total[:, :, :down]
            if hi > COLS:
                gu[...] = total[:, :, down:]

    def gather_rest(p):
        for dz in (2, 6, 1, 7, 0):
            gather_rows(p, dz)

    passing = {
        (A, 0): ((C, dn_y), (AX, up_x), (A, up_z)),
        (A, 1): ((AX, dn_x), (A, dn_z)),
        (A, 2): ((C, dn_y),),
        (B, 0): ((BX, dn_x), (B, dn_z)),
        (B, 1): ((C, up_y), (BX, up_x), (B, up_z)),
        (B, 3): ((C, up_y),),
        (X, 0): ((X, up_z),),
        (X, 1): ((X, dn_z),),
        (AX, 0): ((AX, up_z),),
        (AX, 1): ((AX, dn_z),),
        (BX, 0): ((BX, dn_z),),
        (BX, 1): ((BX, up_z),),
        (C, 0): ((DX, up_x),),
        (C, 1): ((DX, dn_x),),
        (AX, 2): ((DX, dn_y),),
        (BX, 3): ((DX, up_y),),
    }

    def chunk_in(label, n):
        place = region(where[label], chunks[n], c)
        pltpu.make_async_copy(place, place, w_recv.at[label, chunks[n]]).wait()
        for new, target in passing.get((label, n), ()):
            push(place, place, w_recv.at[new, chunks[n]], target)
        push(place, place, sib_recv.at[label, chunks[n]], dev(dc=1))

    def columns(label):
        if label is None:
            loads["w"].wait()
            in_grad(t)
        else:
            sib_arrived(label)
            in_grad(where[label])

    steps = {
        "own_y": lambda n: own_y(chunks[n]),
        "own_x": own_x,
        "tiles": tiles_out,
        "downs": downs_out,
        "tables": tables,
        "slots": slots_out,
        "ring": ring,
        "rest": gather_rest,
        "in": chunk_in,
        "cols": columns,
        "wait_down": wait_down,
    }
    for name, *arg in SEQ:
        steps[name](*arg)

    for cp in sent + g_sent + dn_sent + s_sent + r_sent:
        cp.wait_send()
    for cp in outs:
        cp.wait()


def finish(tmp, *refs):
    ins, outs, bufs, stage, sems = refs[:8], refs[8:15], refs[15:29], refs[29], refs[30]
    step = ROWS // 8
    loads = [pltpu.make_async_copy(ins[i], bufs[i], sems.at[i]) for i in range(8)]
    for i in range(8):
        rows = pl.ds(i * step, step)
        loads.append(pltpu.make_async_copy(tmp.at[rows], stage.at[rows], sems.at[8 + i]))
    for cp in loads:
        cp.start()
    moves = []

    def leave(src, dst):
        cp = pltpu.make_async_copy(src, dst, sems.at[16 + len(moves)])
        cp.start()
        moves.append(cp)

    for cp in loads[:8]:
        cp.wait()
    for half in range(2):
        gr, pr, fi, se = bufs[half * 4 : half * 4 + 4]
        new = adam_update(pr[...], fi[...], se[...], gr[...])
        for i in range(3):
            n = half * 3 + i
            bufs[8 + n][...] = new[i]
            leave(bufs[8 + n], outs[1 + n])
        for i in range(half * 4, half * 4 + 4):
            rows = pl.ds(i * step, step)
            loads[8 + i].wait()
            leave(stage.at[rows], outs[0].at[rows])
    for cp in moves:
        cp.wait()


def body(
    acts, output_gradient, adapter_middle_saved, adapter_per_row, segment_first_row, adapter_per_slot,
    adapter_storage_row, frozen_value_weight, slot_down_matrix, slot_up_matrix, down_matrix_rows,
    down_first_moment, down_second_moment, up_matrix_rows, up_first_moment, up_second_moment,
):
    vmem = pl.BlockSpec(memory_space=pltpu.VMEM)
    smem = pl.BlockSpec(memory_space=pltpu.SMEM)
    hbm = pl.BlockSpec(memory_space=pl.ANY)
    dma = pltpu.SemaphoreType.DMA
    widths = [hi - lo for lo, hi in CUTS]
    n = len(CUTS)

    def each(shape, dtype):
        return [pltpu.VMEM((*shape, width), dtype) for width in widths]

    down_shape, up_shape = (STORED, RANK, COLS), (STORED, RANK, UPC)
    tmp, grad_down, grad_up = pl.pallas_call(
        kernel,
        out_shape=(
            jax.ShapeDtypeStruct((ROWS, WIDTH), BF16),
            jax.ShapeDtypeStruct(down_shape, F32),
            jax.ShapeDtypeStruct(up_shape, F32),
        ),
        in_specs=[hbm, hbm, vmem, vmem, smem, smem, smem, hbm, hbm, hbm],
        out_specs=(hbm, vmem, vmem),
        scratch_shapes=[
            pltpu.VMEM((ROWS, WIDTH), BF16),
            pltpu.VMEM((ROWS, KVW), BF16),
            pltpu.VMEM((SLOTS, RANK, COLS), BF16),
            pltpu.VMEM((SLOTS, RANK, KVW), BF16),
            pltpu.VMEM((8, COLS, KVW), BF16),
            pltpu.VMEM((8, 2 * RANK, COLS), BF16),
            pltpu.VMEM((8, 2 * RANK, COLS), BF16),
            *each((8, 2, RANK), BF16),
            *each((2, 8, 2, RANK), BF16),
            *each((4, SLOTS, RANK), BF16),
            *each((NZ, STORED, RANK), F32),
            *each((4, STORED, RANK), BF16),
            *each((4, STORED, RANK), BF16),
            *each((4, STORED, RANK), BF16),
            *each((4, STORED, RANK), BF16),
            pltpu.VMEM((2 * RANK, ROWS), BF16),
            pltpu.VMEM((ROWS, 2 * RANK), BF16),
            pltpu.VMEM((ROWS, WIDTH), BF16),
            pltpu.SMEM((TILES,), jnp.int32),
            pltpu.SMEM((1, SLOTS), jnp.int32),
            pltpu.SMEM((4 * SLOTS,), jnp.int32),
            pltpu.SMEM((128,), jnp.int32),
            dma((5,)),
            dma((8,)),
            dma((64,)),
            dma((7, 4)),
            dma((7, 4)),
            dma((7,)),
            dma((7,)),
            dma((n, 15)),
            dma((n, 15)),
            dma((n,)),
            dma((n,)),
            dma((n, 8)),
            dma((n, 8)),
            dma((2,)),
        ],
        compiler_params=pltpu.CompilerParams(collective_id=0, has_side_effects=True, vmem_limit_bytes=VMEM_LIMIT),
        cost_estimate=pl.CostEstimate(flops=2 * ROWS * WIDTH * KVW, bytes_accessed=12 << 20, transcendentals=0),
        name="fused",
    )(
        acts, output_gradient, adapter_middle_saved.T, adapter_per_row.reshape(1, ROWS), segment_first_row,
        adapter_per_slot.T, adapter_storage_row, frozen_value_weight, slot_down_matrix[0], slot_up_matrix[0],
    )
    state_down = [jax.ShapeDtypeStruct(down_shape, F32)] * 3
    state_up = [jax.ShapeDtypeStruct(up_shape, F32)] * 3
    return pl.pallas_call(
        finish,
        out_shape=(jax.ShapeDtypeStruct((ROWS, WIDTH), BF16), *state_down, *state_up),
        in_specs=[hbm] * 9,
        out_specs=(hbm,) * 7,
        scratch_shapes=[pltpu.VMEM(down_shape, F32)] * 4
        + [pltpu.VMEM(up_shape, F32)] * 4
        + [pltpu.VMEM(down_shape, F32)] * 3
        + [pltpu.VMEM(up_shape, F32)] * 3
        + [pltpu.VMEM((ROWS, WIDTH), BF16), dma((30,))],
        name="finish",
    )(
        tmp, grad_down, down_matrix_rows, down_first_moment, down_second_moment,
        grad_up, up_matrix_rows, up_first_moment, up_second_moment,
    )


def solution(mesh):
    rows = ("adapter", "tensor")
    stored = P("adapter", None, "tensor")
    in_specs = (
        P(rows, None), P(rows, None), P(rows, None), P(rows), P("adapter", None), P(), P(), P("tensor", None),
        P("adapter", None, None, "tensor"), P("adapter", None, None, None),
        stored, stored, stored, stored, stored, stored,
    )
    out_specs = (P(rows, None),) + (stored,) * 6
    return jax.shard_map(body, mesh=mesh, in_specs=in_specs, out_specs=out_specs, check_vma=False)
```

```python
import jax
import jax.numpy as jnp
from jax import lax
from jax.experimental import pallas as pl
from jax.experimental.pallas import tpu as pltpu
from jax.sharding import PartitionSpec as P

MESH = pl.DeviceIdType.MESH
TILE = 128
STEP = 100
NX, NY, NZ = 4, 4, 8

adapter_scale = 0.5
beta_one = 0.9
beta_two = 0.999
adam_eps = 1e-08
learn_rate = 0.01

ROWS = 256
WIDTH = 8192
KVW = 1024
RANK = 16
SLOTS = 13
TILES = 16
COLS = 1024
UPC = 128
PAY = COLS + UPC
CHUNK = 128
STORED = 4
A, B, C, X, AX, BX, DX = range(7)
CUTS = ((0, 640), (640, PAY))
BLOCK = 256
SUB = 2
VMEM_LIMIT = 56 << 20
SEQ = (
    ("own_y", 0), ("own_y", 1), ("own_x",), ("tables",), ("in", B, 0), ("in", A, 0), ("in", B, 1), ("in", A, 1),
    ("tiles", 0), ("tiles", 1), ("in", X, 0), ("in", AX, 1), ("in", BX, 1), ("in", X, 1), ("in", AX, 0),
    ("in", X, 2), ("in", B, 2), ("downs",), ("cols", None), ("in", BX, 0), ("in", C, 1), ("in", AX, 3),
    ("slots", 0), ("ring", 0, 0), ("rest", 0), ("in", B, 3), ("in", A, 3), ("in", A, 2), ("slots", 1),
    ("in", BX, 3), ("ring", 0, 1), ("ring", 1, 0), ("in", AX, 2), ("in", C, 0), ("ring", 1, 1), ("ring", 2, 0),
    ("rest", 1), ("in", DX, 1), ("ring", 2, 1), ("in", X, 3), ("wait_down",), ("cols", A), ("cols", AX),
    ("in", C, 3), ("ring", 3, 0), ("in", C, 2), ("in", DX, 0), ("in", BX, 2), ("cols", X), ("ring", 3, 1),
    ("cols", B), ("in", DX, 2), ("cols", C), ("in", DX, 3), ("ring", 4, 0), ("cols", BX), ("ring", 4, 1),
    ("cols", DX),
)
F32 = jnp.float32
BF16 = jnp.bfloat16


def adam_update(param, first, second, grad):
    first_new = beta_one * first + (1.0 - beta_one) * grad
    second_new = beta_two * second + (1.0 - beta_two) * grad * grad
    bias_one = 1.0 - beta_one**STEP
    bias_two = 1.0 - beta_two**STEP
    moved = first_new / bias_one / (jnp.sqrt(second_new / bias_two) + adam_eps)
    return (param - learn_rate * moved, first_new, second_new)


def kernel(
    acts_h, og_h, midt, rid, seg, apst, stor, w_h, sd_h, su_h,
    out_h, gd, gu,
    acts, og, sd, su, w, xd, dn,
    gs0, gs1, gr0, gr1, sl0, sl1, dns0, dns1, us0, us1, ur0, ur1, ds0, ds1, dr0, dr1,
    bmt, bm2, ost, tslot, seg2, sr, tab,
    in_sem, out_sem, w_send, w_recv, sib_recv, dn_send, dn_recv, g_send, g_recv,
    s_send, s_recv, r_send, r_recv, m_sem,
):
    gs, gr, sl, dns = (gs0, gs1), (gr0, gr1), (sl0, sl1), (dns0, dns1)
    us, ur, ds, dr = (us0, us1), (ur0, ur1), (ds0, ds1), (dr0, dr1)
    parts = range(len(CUTS))
    a = lax.axis_index("adapter")
    t = lax.axis_index("tensor")
    z, xh, c = a // 4, (a // 2) % 2, a % 2
    y, xl = t // 2, t % 2
    x = xh * 2 + xl

    def dev(dx=0, dy=0, dz=0, dc=0):
        x_, y_, z_, c_ = (x + dx) % NX, (y + dy) % NY, (z + dz) % NZ, (c + dc) % 2
        return (z_ * 4 + (x_ // 2) * 2 + c_, y_ * 2 + x_ % 2)

    def peer(dy, dx, flip=0):
        return (z * 4 + ((xh + flip) % 2) * 2 + c, ((y + dy) % NY) * 2 + (xl + dx) % 2)

    def tensor_of(dy, dx):
        return ((y + dy) % 4) * 2 + (xl + dx) % 2

    loads = {}
    for i, (name, src, dst) in enumerate(
        (
            ("og", og_h, og),
            ("su", su_h, su),
            ("acts", acts_h, acts),
            ("sd", sd_h, sd),
            ("w", w_h, w.at[t]),
        )
    ):
        loads[name] = pltpu.make_async_copy(src, dst, in_sem.at[i])
        loads[name].start()

    plane = [(2, 1), (2, 0), (1, 1), (3, 1), (0, 1), (1, 0), (3, 0), (0, 0)]
    order = [(dy, dx, flip) for dy, dx in plane for flip in (1, 0)]
    barrier = pltpu.get_barrier_semaphore()
    friends = [peer(*d) for d in order[:-1]] + [dev(dz=1), dev(dz=-1), dev(dc=1)]
    for f in friends:
        pl.semaphore_signal(barrier, inc=1, device_id=f, device_id_type=MESH)

    def tile_slot(j, _):
        n = jnp.int32(-1)
        for k in range(SLOTS):
            n = n + (seg[0, k] <= j * TILE).astype(jnp.int32)
        tslot[j] = n
        return 0

    lax.fori_loop(0, TILES, tile_slot, 0)

    loads["og"].wait()
    loads["su"].wait()
    kept = []
    bmt[...] = jnp.zeros_like(bmt)
    for i in range(2):
        slot = tslot[2 * t + i]
        ids = rid[:, i * TILE : (i + 1) * TILE]
        prod = lax.dot_general(
            su[slot], og[i * TILE : (i + 1) * TILE], (((1,), (1,)), ((), ())), preferred_element_type=F32
        )
        own = jnp.where(ids == apst[slot, a], adapter_scale * prod, 0.0)
        bmt[i * RANK : (i + 1) * RANK, i * TILE : (i + 1) * TILE] = own.astype(BF16)
        m = midt[:, i * TILE : (i + 1) * TILE]
        kept.append(jnp.where(ids < stor.shape[0], m, jnp.zeros_like(m)))
    bm2[...] = bmt[...].astype(F32).T.astype(BF16)

    loads["acts"].wait()
    for p in parts:
        lo, hi = CUTS[p]
        down = min(hi, COLS) - lo
        if hi > COLS:
            for i in range(2):
                g = jnp.dot(kept[i], og[i * TILE : (i + 1) * TILE], preferred_element_type=F32)
                g = (adapter_scale * g).astype(BF16)
                for u in range(8):
                    gs[p][u, i, :, down:] = g[:, u * UPC : (u + 1) * UPC]
        for u in range(8):
            for i in range(2):
                block = acts[i * TILE : (i + 1) * TILE, u * COLS + lo : u * COLS + lo + down]
                low = bmt[i * RANK : (i + 1) * RANK, i * TILE : (i + 1) * TILE]
                gs[p][u, i, :, :down] = jnp.dot(low, block, preferred_element_type=F32).astype(BF16)

    pl.semaphore_wait(barrier, len(friends))

    seg_copy = pltpu.make_async_remote_copy(
        src_ref=seg, dst_ref=seg2, send_sem=m_sem.at[0], recv_sem=m_sem.at[1],
        device_id=peer(0, 0, 1), device_id_type=MESH,
    )
    seg_copy.start()

    e = z % 2
    chunks = (2 * e, 2 * e + 1, 2 * (1 - e), 2 * (1 - e) + 1)
    where = {
        A: tensor_of(1, 0), B: tensor_of(3, 0), C: tensor_of(2, 0), X: tensor_of(0, 1),
        AX: tensor_of(1, 1), BX: tensor_of(3, 1), DX: tensor_of(2, 1),
    }
    sent = []

    def region(piece, chunk, half, sub=None):
        rows = CHUNK if sub is None else CHUNK // SUB
        first = half * 512 + chunk * CHUNK + (0 if sub is None else sub * rows)
        return w.at[piece, pl.ds(pl.multiple_of(first, rows), rows)]

    def push(src, dst, sem, target):
        cp = pltpu.make_async_remote_copy(
            src_ref=src, dst_ref=dst, send_sem=w_send.at[len(sent)], recv_sem=sem, device_id=target, device_id_type=MESH
        )
        cp.start()
        sent.append(cp)

    def push_own(chunk, label, sub, target):
        rows = CHUNK // SUB
        src = w_h.at[pl.ds(pl.multiple_of(c * 512 + chunk * CHUNK + sub * rows, rows), rows)]
        push(src, region(t, chunk, c, sub), w_recv.at[label, chunk, sub], target)

    def sib_arrived(label):
        for chunk in range(4):
            place = region(where[label], chunk, 1 - c)
            pltpu.make_async_copy(place, place, sib_recv.at[label, chunk]).wait()

    up_y, dn_y, up_x, dn_x, up_z, dn_z = dev(dy=1), dev(dy=-1), dev(dx=1), dev(dx=-1), dev(dz=1), dev(dz=-1)

    def own_y(chunk):
        for sub in range(SUB):
            push_own(chunk, B, sub, up_y)
            push_own(chunk, A, sub, dn_y)

    def own_x():
        for sub in range(SUB):
            push_own(chunks[0], X, sub, up_x)
            push_own(chunks[1], X, sub, dn_x)

    g_sent = []

    def tiles_out(p):
        for n, (dy, dx, flip) in enumerate(order[:-1]):
            cp = pltpu.make_async_remote_copy(
                src_ref=gs[p].at[tensor_of(dy, dx)], dst_ref=gr[p].at[flip, t],
                send_sem=g_send.at[p, n], recv_sem=g_recv.at[p, n],
                device_id=peer(dy, dx, flip), device_id_type=MESH,
            )
            cp.start()
            g_sent.append(cp)
        gr[p][0, t] = gs[p][t]

    def wait_tiles(p):
        for dy, dx, flip in order[:-1]:
            back = order.index(((4 - dy) % 4, dx, flip))
            place = gr[p].at[flip, tensor_of(dy, dx)]
            pltpu.make_async_copy(place, place, g_recv.at[p, back]).wait()

    dn_sent = []

    def spread(j, _):
        xd[j // 2, pl.ds(pl.multiple_of((j % 2) * RANK, RANK), RANK)] = sd[tslot[j]]
        return 0

    def downs_out():
        loads["sd"].wait()
        lax.fori_loop(0, TILES, spread, 0)
        for n, (dy, dx) in enumerate(plane):
            u = tensor_of(dy, dx)
            if (dy, dx) == (0, 0):
                dn[t] = xd[t]
            else:
                cp = pltpu.make_async_remote_copy(
                    src_ref=xd.at[u], dst_ref=dn.at[t], send_sem=dn_send.at[n], recv_sem=dn_recv.at[n],
                    device_id=peer(dy, dx), device_id_type=MESH,
                )
                cp.start()
                dn_sent.append(cp)

    def wait_down():
        for dy, dx in plane[:-1]:
            place = dn.at[tensor_of(dy, dx)]
            pltpu.make_async_copy(place, place, dn_recv.at[plane.index(((4 - dy) % 4, dx))]).wait()

    outs = []

    def in_grad(piece):
        for j in range(COLS // BLOCK):
            rows = pl.ds(j * BLOCK, BLOCK)
            cols = pl.ds(pl.multiple_of(piece * COLS + j * BLOCK, BLOCK), BLOCK)
            full = lax.dot_general(og[...], w[piece, rows], (((1,), (1,)), ((), ())), preferred_element_type=F32)
            low = jnp.dot(bm2[...], dn[piece, :, rows], preferred_element_type=F32)
            ost[:, cols] = (full + low).astype(BF16)
        cols = pl.ds(pl.multiple_of(piece * COLS, COLS), COLS)
        cp = pltpu.make_async_copy(ost.at[:, cols], out_h.at[:, cols], out_sem.at[len(outs)])
        cp.start()
        outs.append(cp)

    def find(n, _):
        q, rest = n // 32, n % 32
        row = ((z + rest // 4) % NZ) * 16 + xh * 8 + c * 4 + rest % 4
        k_found = jnp.int32(0)
        for k in range(SLOTS):
            k_found = jnp.where(sr[q * SLOTS + k] == row, k + 1, k_found)
        tab[n] = k_found
        return 0

    def tables():
        for q in range(4):
            group = z * 4 + (xh ^ (q % 2)) * 2 + (c ^ (q // 2))
            for k in range(SLOTS):
                sr[q * SLOTS + k] = stor[apst[k, group]]
        lax.fori_loop(0, 128, find, 0)

    s_sent = []

    def slots_out(p):
        if p == 0:
            seg_copy.wait()
        wait_tiles(p)
        for q, table in ((0, seg), (1, seg2)):
            for k in range(SLOTS):
                first = table[0, k] // TILE
                last = table[0, k + 1] // TILE if k + 1 < SLOTS else TILES
                total = jnp.zeros((RANK, sl[p].shape[-1]), F32)
                for i in range(4):
                    j = jnp.minimum(first + i, TILES - 1)
                    total = total + jnp.where(first + i < last, gr[p][q, j // 2, j % 2].astype(F32), 0.0)
                sl[p][q, k] = total.astype(BF16)
        cp = pltpu.make_async_remote_copy(
            src_ref=sl[p].at[pl.ds(0, 2)], dst_ref=sl[p].at[pl.ds(2, 2)], send_sem=s_send.at[p], recv_sem=s_recv.at[p],
            device_id=dev(dc=1), device_id_type=MESH,
        )
        cp.start()
        s_sent.append(cp)

    def gather_rows(p, dz):
        def one(r, _):
            total = jnp.zeros((RANK, sl[p].shape[-1]), F32)
            for q in range(4):
                k = tab[q * 32 + dz * 4 + r]
                total = total + jnp.where(k > 0, sl[p][q, jnp.maximum(k - 1, 0)].astype(F32), 0.0)
            dns[p][dz, r] = total
            return 0

        lax.fori_loop(0, STORED, one, 0)

    r_sent = []

    def ring_send(src, dst, p, direction, step):
        n = direction * 4 + step
        cp = pltpu.make_async_remote_copy(
            src_ref=src, dst_ref=dst, send_sem=r_send.at[p, n], recv_sem=r_recv.at[p, n],
            device_id=dn_z if direction else up_z, device_id_type=MESH,
        )
        cp.start()
        r_sent.append(cp)

    def ring_wait(ref, p, direction, step):
        pltpu.make_async_copy(ref, ref, r_recv.at[p, direction * 4 + step]).wait()

    def ring(step, p):
        if step == 0:
            place = sl[p].at[pl.ds(2, 2)]
            pltpu.make_async_copy(place, place, s_recv.at[p]).wait()
            gather_rows(p, 4)
            us[p][0, 0:2] = dns[p][4, 0:2].astype(BF16)
            ring_send(us[p].at[0, pl.ds(0, 2)], ur[p].at[0, pl.ds(0, 2)], p, 0, 0)
            ds[p][0, 2:4] = dns[p][4, 2:4].astype(BF16)
            ring_send(ds[p].at[0, pl.ds(2, 2)], dr[p].at[0, pl.ds(2, 2)], p, 1, 0)
            gather_rows(p, 3)
            gather_rows(p, 5)
        elif step == 1:
            ring_wait(ur[p].at[0, pl.ds(0, 2)], p, 0, 0)
            us[p][1, 0:2] = (dns[p][3, 0:2] + ur[p][0, 0:2].astype(F32)).astype(BF16)
            us[p][1, 2:4] = dns[p][3, 2:4].astype(BF16)
            ring_send(us[p].at[1], ur[p].at[1], p, 0, 1)
            ring_wait(dr[p].at[0, pl.ds(2, 2)], p, 1, 0)
            ds[p][1, 0:2] = dns[p][5, 0:2].astype(BF16)
            ds[p][1, 2:4] = (dns[p][5, 2:4] + dr[p][0, 2:4].astype(F32)).astype(BF16)
            ring_send(ds[p].at[1], dr[p].at[1], p, 1, 1)
        elif step < 4:
            ring_wait(ur[p].at[step - 1], p, 0, step - 1)
            us[p][step] = (dns[p][4 - step] + ur[p][step - 1].astype(F32)).astype(BF16)
            ring_send(us[p].at[step], ur[p].at[step], p, 0, step)
            ring_wait(dr[p].at[step - 1], p, 1, step - 1)
            ds[p][step] = (dns[p][4 + step] + dr[p][step - 1].astype(F32)).astype(BF16)
            ring_send(ds[p].at[step], dr[p].at[step], p, 1, step)
        else:
            ring_wait(ur[p].at[3], p, 0, 3)
            ring_wait(dr[p].at[3], p, 1, 3)
            total = dns[p][0] + ur[p][3].astype(F32) + dr[p][3].astype(F32)
            lo, hi = CUTS[p]
            down = min(hi, COLS) - lo
            gd[:, :, lo : lo + down] = total[:, :, :down]
            if hi > COLS:
                gu[...] = total[:, :, down:]

    def gather_rest(p):
        for dz in (2, 6, 1, 7, 0):
            gather_rows(p, dz)

    passing = {
        (A, 0): ((C, dn_y), (AX, up_x), (A, up_z)),
        (A, 1): ((AX, dn_x), (A, dn_z)),
        (A, 2): ((C, dn_y),),
        (B, 0): ((BX, dn_x), (B, dn_z)),
        (B, 1): ((C, up_y), (BX, up_x), (B, up_z)),
        (B, 3): ((C, up_y),),
        (X, 0): ((X, up_z),),
        (X, 1): ((X, dn_z),),
        (AX, 0): ((AX, up_z),),
        (AX, 1): ((AX, dn_z),),
        (BX, 0): ((BX, dn_z),),
        (BX, 1): ((BX, up_z),),
        (C, 0): ((DX, up_x),),
        (C, 1): ((DX, dn_x),),
        (AX, 2): ((DX, dn_y),),
        (BX, 3): ((DX, up_y),),
    }

    def chunk_in(label, n):
        for sub in range(SUB):
            place = region(where[label], chunks[n], c, sub)
            pltpu.make_async_copy(place, place, w_recv.at[label, chunks[n], sub]).wait()
            for new, target in passing.get((label, n), ()):
                push(place, place, w_recv.at[new, chunks[n], sub], target)
        place = region(where[label], chunks[n], c)
        push(place, place, sib_recv.at[label, chunks[n]], dev(dc=1))

    def columns(label):
        if label is None:
            loads["w"].wait()
            in_grad(t)
        else:
            sib_arrived(label)
            in_grad(where[label])

    steps = {
        "own_y": lambda n: own_y(chunks[n]),
        "own_x": own_x,
        "tiles": tiles_out,
        "downs": downs_out,
        "tables": tables,
        "slots": slots_out,
        "ring": ring,
        "rest": gather_rest,
        "in": chunk_in,
        "cols": columns,
        "wait_down": wait_down,
    }
    for name, *arg in SEQ:
        steps[name](*arg)

    for cp in sent + g_sent + dn_sent + s_sent + r_sent:
        cp.wait_send()
    for cp in outs:
        cp.wait()


def finish(tmp, *refs):
    ins, outs, bufs, stage, sems = refs[:8], refs[8:15], refs[15:29], refs[29], refs[30]
    step = ROWS // 8
    loads = [pltpu.make_async_copy(ins[i], bufs[i], sems.at[i]) for i in range(8)]
    for i in range(8):
        rows = pl.ds(i * step, step)
        loads.append(pltpu.make_async_copy(tmp.at[rows], stage.at[rows], sems.at[8 + i]))
    for cp in loads:
        cp.start()
    moves = []

    def leave(src, dst):
        cp = pltpu.make_async_copy(src, dst, sems.at[16 + len(moves)])
        cp.start()
        moves.append(cp)

    for cp in loads[:8]:
        cp.wait()
    for half in range(2):
        gr, pr, fi, se = bufs[half * 4 : half * 4 + 4]
        new = adam_update(pr[...], fi[...], se[...], gr[...])
        for i in range(3):
            n = half * 3 + i
            bufs[8 + n][...] = new[i]
            leave(bufs[8 + n], outs[1 + n])
        for i in range(half * 4, half * 4 + 4):
            rows = pl.ds(i * step, step)
            loads[8 + i].wait()
            leave(stage.at[rows], outs[0].at[rows])
    for cp in moves:
        cp.wait()


def body(
    acts, output_gradient, adapter_middle_saved, adapter_per_row, segment_first_row, adapter_per_slot,
    adapter_storage_row, frozen_value_weight, slot_down_matrix, slot_up_matrix, down_matrix_rows,
    down_first_moment, down_second_moment, up_matrix_rows, up_first_moment, up_second_moment,
):
    vmem = pl.BlockSpec(memory_space=pltpu.VMEM)
    smem = pl.BlockSpec(memory_space=pltpu.SMEM)
    hbm = pl.BlockSpec(memory_space=pl.ANY)
    dma = pltpu.SemaphoreType.DMA
    widths = [hi - lo for lo, hi in CUTS]
    n = len(CUTS)

    def each(shape, dtype):
        return [pltpu.VMEM((*shape, width), dtype) for width in widths]

    down_shape, up_shape = (STORED, RANK, COLS), (STORED, RANK, UPC)
    tmp, grad_down, grad_up = pl.pallas_call(
        kernel,
        out_shape=(
            jax.ShapeDtypeStruct((ROWS, WIDTH), BF16),
            jax.ShapeDtypeStruct(down_shape, F32),
            jax.ShapeDtypeStruct(up_shape, F32),
        ),
        in_specs=[hbm, hbm, vmem, vmem, smem, smem, smem, hbm, hbm, hbm],
        out_specs=(hbm, vmem, vmem),
        scratch_shapes=[
            pltpu.VMEM((ROWS, WIDTH), BF16),
            pltpu.VMEM((ROWS, KVW), BF16),
            pltpu.VMEM((SLOTS, RANK, COLS), BF16),
            pltpu.VMEM((SLOTS, RANK, KVW), BF16),
            pltpu.VMEM((8, COLS, KVW), BF16),
            pltpu.VMEM((8, 2 * RANK, COLS), BF16),
            pltpu.VMEM((8, 2 * RANK, COLS), BF16),
            *each((8, 2, RANK), BF16),
            *each((2, 8, 2, RANK), BF16),
            *each((4, SLOTS, RANK), BF16),
            *each((NZ, STORED, RANK), F32),
            *each((4, STORED, RANK), BF16),
            *each((4, STORED, RANK), BF16),
            *each((4, STORED, RANK), BF16),
            *each((4, STORED, RANK), BF16),
            pltpu.VMEM((2 * RANK, ROWS), BF16),
            pltpu.VMEM((ROWS, 2 * RANK), BF16),
            pltpu.VMEM((ROWS, WIDTH), BF16),
            pltpu.SMEM((TILES,), jnp.int32),
            pltpu.SMEM((1, SLOTS), jnp.int32),
            pltpu.SMEM((4 * SLOTS,), jnp.int32),
            pltpu.SMEM((128,), jnp.int32),
            dma((5,)),
            dma((8,)),
            dma((28 * (SUB + 1),)),
            dma((7, 4, SUB)),
            dma((7, 4)),
            dma((7,)),
            dma((7,)),
            dma((n, 15)),
            dma((n, 15)),
            dma((n,)),
            dma((n,)),
            dma((n, 8)),
            dma((n, 8)),
            dma((2,)),
        ],
        compiler_params=pltpu.CompilerParams(collective_id=0, has_side_effects=True, vmem_limit_bytes=VMEM_LIMIT),
        cost_estimate=pl.CostEstimate(flops=2 * ROWS * WIDTH * KVW, bytes_accessed=12 << 20, transcendentals=0),
        name="fused",
    )(
        acts, output_gradient, adapter_middle_saved.T, adapter_per_row.reshape(1, ROWS), segment_first_row,
        adapter_per_slot.T, adapter_storage_row, frozen_value_weight, slot_down_matrix[0], slot_up_matrix[0],
    )
    state_down = [jax.ShapeDtypeStruct(down_shape, F32)] * 3
    state_up = [jax.ShapeDtypeStruct(up_shape, F32)] * 3
    return pl.pallas_call(
        finish,
        out_shape=(jax.ShapeDtypeStruct((ROWS, WIDTH), BF16), *state_down, *state_up),
        in_specs=[hbm] * 9,
        out_specs=(hbm,) * 7,
        scratch_shapes=[pltpu.VMEM(down_shape, F32)] * 4
        + [pltpu.VMEM(up_shape, F32)] * 4
        + [pltpu.VMEM(down_shape, F32)] * 3
        + [pltpu.VMEM(up_shape, F32)] * 3
        + [pltpu.VMEM((ROWS, WIDTH), BF16), dma((30,))],
        name="finish",
    )(
        tmp, grad_down, down_matrix_rows, down_first_moment, down_second_moment,
        grad_up, up_matrix_rows, up_first_moment, up_second_moment,
    )


def solution(mesh):
    rows = ("adapter", "tensor")
    stored = P("adapter", None, "tensor")
    in_specs = (
        P(rows, None), P(rows, None), P(rows, None), P(rows), P("adapter", None), P(), P(), P("tensor", None),
        P("adapter", None, None, "tensor"), P("adapter", None, None, None),
        stored, stored, stored, stored, stored, stored,
    )
    out_specs = (P(rows, None),) + (stored,) * 6
    return jax.shard_map(body, mesh=mesh, in_specs=in_specs, out_specs=out_specs, check_vma=False)
```

```python
import jax
import jax.numpy as jnp
from jax import lax
from jax.experimental import pallas as pl
from jax.experimental.pallas import tpu as pltpu
from jax.sharding import PartitionSpec as P

MESH = pl.DeviceIdType.MESH
TILE = 128
STEP = 100
NX, NY, NZ = 4, 4, 8

adapter_scale = 0.5
beta_one = 0.9
beta_two = 0.999
adam_eps = 1e-08
learn_rate = 0.01

ROWS = 256
WIDTH = 8192
KVW = 1024
RANK = 16
SLOTS = 13
TILES = 16
COLS = 1024
UPC = 128
PAY = COLS + UPC
CHUNK = 128
STORED = 4
A, B, C, X, AX, BX, DX = range(7)
CUTS = ((0, 640), (640, PAY))
BLOCK = 256
SUB = 2
VMEM_LIMIT = 58 << 20
SEQ = (
    ("own_y", 0), ("own_y", 1), ("own_x",), ("tables",), ("in", B, 0), ("in", A, 0), ("in", B, 1), ("in", A, 1),
    ("tiles", 0), ("tiles", 1), ("in", X, 0), ("in", AX, 1), ("in", BX, 1), ("in", X, 1), ("in", AX, 0),
    ("in", X, 2), ("in", B, 2), ("downs",), ("cols", None), ("in", BX, 0), ("in", C, 1), ("in", AX, 3),
    ("slots", 0), ("ring", 0, 0), ("rest", 0), ("in", B, 3), ("in", A, 3), ("in", A, 2), ("slots", 1),
    ("in", BX, 3), ("ring", 0, 1), ("ring", 1, 0), ("in", AX, 2), ("in", C, 0), ("ring", 1, 1), ("ring", 2, 0),
    ("rest", 1), ("in", DX, 1), ("ring", 2, 1), ("in", X, 3), ("wait_down",), ("cols", A), ("cols", AX),
    ("in", C, 3), ("ring", 3, 0), ("in", C, 2), ("in", DX, 0), ("in", BX, 2), ("cols", X), ("ring", 3, 1),
    ("cols", B), ("in", DX, 2), ("cols", C), ("in", DX, 3), ("ring", 4, 0), ("cols", BX), ("ring", 4, 1),
    ("cols", DX),
)
F32 = jnp.float32
BF16 = jnp.bfloat16


def adam_update(param, first, second, grad):
    first_new = beta_one * first + (1.0 - beta_one) * grad
    second_new = beta_two * second + (1.0 - beta_two) * grad * grad
    bias_one = 1.0 - beta_one**STEP
    bias_two = 1.0 - beta_two**STEP
    moved = first_new / bias_one / (jnp.sqrt(second_new / bias_two) + adam_eps)
    return (param - learn_rate * moved, first_new, second_new)


def kernel(
    acts_h, og_h, midt, rid, seg, apst, stor, w_h, sd_h, su_h,
    out, gd, gu,
    acts, og, sd, su, w, xd, dn,
    gs0, gs1, gr0, gr1, sl0, sl1, dns0, dns1, us0, us1, ur0, ur1, ds0, ds1, dr0, dr1,
    bmt, bm2, tslot, seg2, sr, tab,
    in_sem, w_send, w_recv, sib_recv, dn_send, dn_recv, g_send, g_recv,
    s_send, s_recv, r_send, r_recv, m_sem,
):
    gs, gr, sl, dns = (gs0, gs1), (gr0, gr1), (sl0, sl1), (dns0, dns1)
    us, ur, ds, dr = (us0, us1), (ur0, ur1), (ds0, ds1), (dr0, dr1)
    parts = range(len(CUTS))
    a = lax.axis_index("adapter")
    t = lax.axis_index("tensor")
    z, xh, c = a // 4, (a // 2) % 2, a % 2
    y, xl = t // 2, t % 2
    x = xh * 2 + xl

    def dev(dx=0, dy=0, dz=0, dc=0):
        x_, y_, z_, c_ = (x + dx) % NX, (y + dy) % NY, (z + dz) % NZ, (c + dc) % 2
        return (z_ * 4 + (x_ // 2) * 2 + c_, y_ * 2 + x_ % 2)

    def peer(dy, dx, flip=0):
        return (z * 4 + ((xh + flip) % 2) * 2 + c, ((y + dy) % NY) * 2 + (xl + dx) % 2)

    def tensor_of(dy, dx):
        return ((y + dy) % 4) * 2 + (xl + dx) % 2

    loads = {}
    for i, (name, src, dst) in enumerate(
        (
            ("og", og_h, og),
            ("su", su_h, su),
            ("acts", acts_h, acts),
            ("sd", sd_h, sd),
            ("w", w_h, w.at[t]),
        )
    ):
        loads[name] = pltpu.make_async_copy(src, dst, in_sem.at[i])
        loads[name].start()

    plane = [(2, 1), (2, 0), (1, 1), (3, 1), (0, 1), (1, 0), (3, 0), (0, 0)]
    order = [(dy, dx, flip) for dy, dx in plane for flip in (1, 0)]
    barrier = pltpu.get_barrier_semaphore()
    friends = [peer(*d) for d in order[:-1]] + [dev(dz=1), dev(dz=-1), dev(dc=1)]
    for f in friends:
        pl.semaphore_signal(barrier, inc=1, device_id=f, device_id_type=MESH)

    def tile_slot(j, _):
        n = jnp.int32(-1)
        for k in range(SLOTS):
            n = n + (seg[0, k] <= j * TILE).astype(jnp.int32)
        tslot[j] = n
        return 0

    lax.fori_loop(0, TILES, tile_slot, 0)

    loads["og"].wait()
    loads["su"].wait()
    kept = []
    bmt[...] = jnp.zeros_like(bmt)
    for i in range(2):
        slot = tslot[2 * t + i]
        ids = rid[:, i * TILE : (i + 1) * TILE]
        prod = lax.dot_general(
            su[slot], og[i * TILE : (i + 1) * TILE], (((1,), (1,)), ((), ())), preferred_element_type=F32
        )
        own = jnp.where(ids == apst[slot, a], adapter_scale * prod, 0.0)
        bmt[i * RANK : (i + 1) * RANK, i * TILE : (i + 1) * TILE] = own.astype(BF16)
        m = midt[:, i * TILE : (i + 1) * TILE]
        kept.append(jnp.where(ids < stor.shape[0], m, jnp.zeros_like(m)))
    bm2[...] = bmt[...].astype(F32).T.astype(BF16)

    loads["acts"].wait()
    for p in parts:
        lo, hi = CUTS[p]
        down = min(hi, COLS) - lo
        if hi > COLS:
            for i in range(2):
                g = jnp.dot(kept[i], og[i * TILE : (i + 1) * TILE], preferred_element_type=F32)
                g = (adapter_scale * g).astype(BF16)
                for u in range(8):
                    gs[p][u, i, :, down:] = g[:, u * UPC : (u + 1) * UPC]
        for u in range(8):
            for i in range(2):
                block = acts[i * TILE : (i + 1) * TILE, u * COLS + lo : u * COLS + lo + down]
                low = bmt[i * RANK : (i + 1) * RANK, i * TILE : (i + 1) * TILE]
                gs[p][u, i, :, :down] = jnp.dot(low, block, preferred_element_type=F32).astype(BF16)

    pl.semaphore_wait(barrier, len(friends))

    seg_copy = pltpu.make_async_remote_copy(
        src_ref=seg, dst_ref=seg2, send_sem=m_sem.at[0], recv_sem=m_sem.at[1],
        device_id=peer(0, 0, 1), device_id_type=MESH,
    )
    seg_copy.start()

    e = z % 2
    chunks = (2 * e, 2 * e + 1, 2 * (1 - e), 2 * (1 - e) + 1)
    where = {
        A: tensor_of(1, 0), B: tensor_of(3, 0), C: tensor_of(2, 0), X: tensor_of(0, 1),
        AX: tensor_of(1, 1), BX: tensor_of(3, 1), DX: tensor_of(2, 1),
    }
    sent = []

    def region(piece, chunk, half, sub=None):
        rows = CHUNK if sub is None else CHUNK // SUB
        first = half * 512 + chunk * CHUNK + (0 if sub is None else sub * rows)
        return w.at[piece, pl.ds(pl.multiple_of(first, rows), rows)]

    def push(src, dst, sem, target):
        cp = pltpu.make_async_remote_copy(
            src_ref=src, dst_ref=dst, send_sem=w_send.at[len(sent)], recv_sem=sem, device_id=target, device_id_type=MESH
        )
        cp.start()
        sent.append(cp)

    def push_own(chunk, label, sub, target):
        rows = CHUNK // SUB
        src = w_h.at[pl.ds(pl.multiple_of(c * 512 + chunk * CHUNK + sub * rows, rows), rows)]
        push(src, region(t, chunk, c, sub), w_recv.at[label, chunk, sub], target)

    def sib_arrived(label):
        for chunk in range(4):
            place = region(where[label], chunk, 1 - c)
            pltpu.make_async_copy(place, place, sib_recv.at[label, chunk]).wait()

    up_y, dn_y, up_x, dn_x, up_z, dn_z = dev(dy=1), dev(dy=-1), dev(dx=1), dev(dx=-1), dev(dz=1), dev(dz=-1)

    def own_y(chunk):
        for sub in range(SUB):
            push_own(chunk, B, sub, up_y)
            push_own(chunk, A, sub, dn_y)

    def own_x():
        for sub in range(SUB):
            push_own(chunks[0], X, sub, up_x)
            push_own(chunks[1], X, sub, dn_x)

    g_sent = []

    def tiles_out(p):
        for n, (dy, dx, flip) in enumerate(order[:-1]):
            cp = pltpu.make_async_remote_copy(
                src_ref=gs[p].at[tensor_of(dy, dx)], dst_ref=gr[p].at[flip, t],
                send_sem=g_send.at[p, n], recv_sem=g_recv.at[p, n],
                device_id=peer(dy, dx, flip), device_id_type=MESH,
            )
            cp.start()
            g_sent.append(cp)
        gr[p][0, t] = gs[p][t]

    def wait_tiles(p):
        for dy, dx, flip in order[:-1]:
            back = order.index(((4 - dy) % 4, dx, flip))
            place = gr[p].at[flip, tensor_of(dy, dx)]
            pltpu.make_async_copy(place, place, g_recv.at[p, back]).wait()

    dn_sent = []

    def spread(j, _):
        xd[j // 2, pl.ds(pl.multiple_of((j % 2) * RANK, RANK), RANK)] = sd[tslot[j]]
        return 0

    def downs_out():
        loads["sd"].wait()
        lax.fori_loop(0, TILES, spread, 0)
        for n, (dy, dx) in enumerate(plane):
            u = tensor_of(dy, dx)
            if (dy, dx) == (0, 0):
                dn[t] = xd[t]
            else:
                cp = pltpu.make_async_remote_copy(
                    src_ref=xd.at[u], dst_ref=dn.at[t], send_sem=dn_send.at[n], recv_sem=dn_recv.at[n],
                    device_id=peer(dy, dx), device_id_type=MESH,
                )
                cp.start()
                dn_sent.append(cp)

    def wait_down():
        for dy, dx in plane[:-1]:
            place = dn.at[tensor_of(dy, dx)]
            pltpu.make_async_copy(place, place, dn_recv.at[plane.index(((4 - dy) % 4, dx))]).wait()

    def in_grad(piece):
        for j in range(COLS // BLOCK):
            rows = pl.ds(j * BLOCK, BLOCK)
            cols = pl.ds(pl.multiple_of(piece * COLS + j * BLOCK, BLOCK), BLOCK)
            full = lax.dot_general(og[...], w[piece, rows], (((1,), (1,)), ((), ())), preferred_element_type=F32)
            low = jnp.dot(bm2[...], dn[piece, :, rows], preferred_element_type=F32)
            out[:, cols] = (full + low).astype(BF16)

    def find(n, _):
        q, rest = n // 32, n % 32
        row = ((z + rest // 4) % NZ) * 16 + xh * 8 + c * 4 + rest % 4
        k_found = jnp.int32(0)
        for k in range(SLOTS):
            k_found = jnp.where(sr[q * SLOTS + k] == row, k + 1, k_found)
        tab[n] = k_found
        return 0

    def tables():
        for q in range(4):
            group = z * 4 + (xh ^ (q % 2)) * 2 + (c ^ (q // 2))
            for k in range(SLOTS):
                sr[q * SLOTS + k] = stor[apst[k, group]]
        lax.fori_loop(0, 128, find, 0)

    s_sent = []

    def slots_out(p):
        if p == 0:
            seg_copy.wait()
        wait_tiles(p)
        for q, table in ((0, seg), (1, seg2)):
            for k in range(SLOTS):
                first = table[0, k] // TILE
                last = table[0, k + 1] // TILE if k + 1 < SLOTS else TILES
                total = jnp.zeros((RANK, sl[p].shape[-1]), F32)
                for i in range(4):
                    j = jnp.minimum(first + i, TILES - 1)
                    total = total + jnp.where(first + i < last, gr[p][q, j // 2, j % 2].astype(F32), 0.0)
                sl[p][q, k] = total.astype(BF16)
        cp = pltpu.make_async_remote_copy(
            src_ref=sl[p].at[pl.ds(0, 2)], dst_ref=sl[p].at[pl.ds(2, 2)], send_sem=s_send.at[p], recv_sem=s_recv.at[p],
            device_id=dev(dc=1), device_id_type=MESH,
        )
        cp.start()
        s_sent.append(cp)

    def gather_rows(p, dz):
        def one(r, _):
            total = jnp.zeros((RANK, sl[p].shape[-1]), F32)
            for q in range(4):
                k = tab[q * 32 + dz * 4 + r]
                total = total + jnp.where(k > 0, sl[p][q, jnp.maximum(k - 1, 0)].astype(F32), 0.0)
            dns[p][dz, r] = total
            return 0

        lax.fori_loop(0, STORED, one, 0)

    r_sent = []

    def ring_send(src, dst, p, direction, step):
        n = direction * 4 + step
        cp = pltpu.make_async_remote_copy(
            src_ref=src, dst_ref=dst, send_sem=r_send.at[p, n], recv_sem=r_recv.at[p, n],
            device_id=dn_z if direction else up_z, device_id_type=MESH,
        )
        cp.start()
        r_sent.append(cp)

    def ring_wait(ref, p, direction, step):
        pltpu.make_async_copy(ref, ref, r_recv.at[p, direction * 4 + step]).wait()

    def ring(step, p):
        if step == 0:
            place = sl[p].at[pl.ds(2, 2)]
            pltpu.make_async_copy(place, place, s_recv.at[p]).wait()
            gather_rows(p, 4)
            us[p][0, 0:2] = dns[p][4, 0:2].astype(BF16)
            ring_send(us[p].at[0, pl.ds(0, 2)], ur[p].at[0, pl.ds(0, 2)], p, 0, 0)
            ds[p][0, 2:4] = dns[p][4, 2:4].astype(BF16)
            ring_send(ds[p].at[0, pl.ds(2, 2)], dr[p].at[0, pl.ds(2, 2)], p, 1, 0)
            gather_rows(p, 3)
            gather_rows(p, 5)
        elif step == 1:
            ring_wait(ur[p].at[0, pl.ds(0, 2)], p, 0, 0)
            us[p][1, 0:2] = (dns[p][3, 0:2] + ur[p][0, 0:2].astype(F32)).astype(BF16)
            us[p][1, 2:4] = dns[p][3, 2:4].astype(BF16)
            ring_send(us[p].at[1], ur[p].at[1], p, 0, 1)
            ring_wait(dr[p].at[0, pl.ds(2, 2)], p, 1, 0)
            ds[p][1, 0:2] = dns[p][5, 0:2].astype(BF16)
            ds[p][1, 2:4] = (dns[p][5, 2:4] + dr[p][0, 2:4].astype(F32)).astype(BF16)
            ring_send(ds[p].at[1], dr[p].at[1], p, 1, 1)
        elif step < 4:
            ring_wait(ur[p].at[step - 1], p, 0, step - 1)
            us[p][step] = (dns[p][4 - step] + ur[p][step - 1].astype(F32)).astype(BF16)
            ring_send(us[p].at[step], ur[p].at[step], p, 0, step)
            ring_wait(dr[p].at[step - 1], p, 1, step - 1)
            ds[p][step] = (dns[p][4 + step] + dr[p][step - 1].astype(F32)).astype(BF16)
            ring_send(ds[p].at[step], dr[p].at[step], p, 1, step)
        else:
            ring_wait(ur[p].at[3], p, 0, 3)
            ring_wait(dr[p].at[3], p, 1, 3)
            total = dns[p][0] + ur[p][3].astype(F32) + dr[p][3].astype(F32)
            lo, hi = CUTS[p]
            down = min(hi, COLS) - lo
            gd[:, :, lo : lo + down] = total[:, :, :down]
            if hi > COLS:
                gu[...] = total[:, :, down:]

    def gather_rest(p):
        for dz in (2, 6, 1, 7, 0):
            gather_rows(p, dz)

    passing = {
        (A, 0): ((C, dn_y), (AX, up_x), (A, up_z)),
        (A, 1): ((AX, dn_x), (A, dn_z)),
        (A, 2): ((C, dn_y),),
        (B, 0): ((BX, dn_x), (B, dn_z)),
        (B, 1): ((C, up_y), (BX, up_x), (B, up_z)),
        (B, 3): ((C, up_y),),
        (X, 0): ((X, up_z),),
        (X, 1): ((X, dn_z),),
        (AX, 0): ((AX, up_z),),
        (AX, 1): ((AX, dn_z),),
        (BX, 0): ((BX, dn_z),),
        (BX, 1): ((BX, up_z),),
        (C, 0): ((DX, up_x),),
        (C, 1): ((DX, dn_x),),
        (AX, 2): ((DX, dn_y),),
        (BX, 3): ((DX, up_y),),
    }

    def chunk_in(label, n):
        for sub in range(SUB):
            place = region(where[label], chunks[n], c, sub)
            pltpu.make_async_copy(place, place, w_recv.at[label, chunks[n], sub]).wait()
            for new, target in passing.get((label, n), ()):
                push(place, place, w_recv.at[new, chunks[n], sub], target)
        place = region(where[label], chunks[n], c)
        push(place, place, sib_recv.at[label, chunks[n]], dev(dc=1))

    def columns(label):
        if label is None:
            loads["w"].wait()
            in_grad(t)
        else:
            sib_arrived(label)
            in_grad(where[label])

    steps = {
        "own_y": lambda n: own_y(chunks[n]),
        "own_x": own_x,
        "tiles": tiles_out,
        "downs": downs_out,
        "tables": tables,
        "slots": slots_out,
        "ring": ring,
        "rest": gather_rest,
        "in": chunk_in,
        "cols": columns,
        "wait_down": wait_down,
    }
    for name, *arg in SEQ:
        steps[name](*arg)

    for cp in sent + g_sent + dn_sent + s_sent + r_sent:
        cp.wait_send()


def finish(tmp, grad_down, *refs):
    states, grad_up, outs, bufs, sems = refs[:3], refs[3], refs[7:14], refs[14:26], refs[26]
    states += refs[4:7]
    loads = [pltpu.make_async_copy(states[i], bufs[i], sems.at[i]) for i in range(6)]
    for cp in loads:
        cp.start()
    moves = []

    def leave(src, dst):
        cp = pltpu.make_async_copy(src, dst, sems.at[6 + len(moves)])
        cp.start()
        moves.append(cp)

    step = ROWS // 8
    for i in range(8):
        rows = pl.ds(i * step, step)
        leave(tmp.at[rows], outs[0].at[rows])
    for cp in loads:
        cp.wait()
    for half, grad in enumerate((grad_down, grad_up)):
        new = adam_update(*(ref[...] for ref in bufs[half * 3 : half * 3 + 3]), grad[...])
        for i in range(3):
            n = half * 3 + i
            bufs[6 + n][...] = new[i]
            leave(bufs[6 + n], outs[1 + n])
    for cp in moves:
        cp.wait()


def body(
    acts, output_gradient, adapter_middle_saved, adapter_per_row, segment_first_row, adapter_per_slot,
    adapter_storage_row, frozen_value_weight, slot_down_matrix, slot_up_matrix, down_matrix_rows,
    down_first_moment, down_second_moment, up_matrix_rows, up_first_moment, up_second_moment,
):
    vmem = pl.BlockSpec(memory_space=pltpu.VMEM)
    smem = pl.BlockSpec(memory_space=pltpu.SMEM)
    hbm = pl.BlockSpec(memory_space=pl.ANY)
    dma = pltpu.SemaphoreType.DMA
    widths = [hi - lo for lo, hi in CUTS]
    n = len(CUTS)

    def each(shape, dtype):
        return [pltpu.VMEM((*shape, width), dtype) for width in widths]

    down_shape, up_shape = (STORED, RANK, COLS), (STORED, RANK, UPC)
    tmp, grad_down, grad_up = pl.pallas_call(
        kernel,
        out_shape=(
            pltpu.VMEM((ROWS, WIDTH), BF16),
            pltpu.VMEM(down_shape, F32),
            pltpu.VMEM(up_shape, F32),
        ),
        in_specs=[hbm, hbm, vmem, vmem, smem, smem, smem, hbm, hbm, hbm],
        out_specs=(vmem, vmem, vmem),
        scratch_shapes=[
            pltpu.VMEM((ROWS, WIDTH), BF16),
            pltpu.VMEM((ROWS, KVW), BF16),
            pltpu.VMEM((SLOTS, RANK, COLS), BF16),
            pltpu.VMEM((SLOTS, RANK, KVW), BF16),
            pltpu.VMEM((8, COLS, KVW), BF16),
            pltpu.VMEM((8, 2 * RANK, COLS), BF16),
            pltpu.VMEM((8, 2 * RANK, COLS), BF16),
            *each((8, 2, RANK), BF16),
            *each((2, 8, 2, RANK), BF16),
            *each((4, SLOTS, RANK), BF16),
            *each((NZ, STORED, RANK), F32),
            *each((4, STORED, RANK), BF16),
            *each((4, STORED, RANK), BF16),
            *each((4, STORED, RANK), BF16),
            *each((4, STORED, RANK), BF16),
            pltpu.VMEM((2 * RANK, ROWS), BF16),
            pltpu.VMEM((ROWS, 2 * RANK), BF16),
            pltpu.SMEM((TILES,), jnp.int32),
            pltpu.SMEM((1, SLOTS), jnp.int32),
            pltpu.SMEM((4 * SLOTS,), jnp.int32),
            pltpu.SMEM((128,), jnp.int32),
            dma((5,)),
            dma((28 * (SUB + 1),)),
            dma((7, 4, SUB)),
            dma((7, 4)),
            dma((7,)),
            dma((7,)),
            dma((n, 15)),
            dma((n, 15)),
            dma((n,)),
            dma((n,)),
            dma((n, 8)),
            dma((n, 8)),
            dma((2,)),
        ],
        compiler_params=pltpu.CompilerParams(collective_id=0, has_side_effects=True, vmem_limit_bytes=VMEM_LIMIT),
        cost_estimate=pl.CostEstimate(flops=2 * ROWS * WIDTH * KVW, bytes_accessed=12 << 20, transcendentals=0),
        name="fused",
    )(
        acts, output_gradient, adapter_middle_saved.T, adapter_per_row.reshape(1, ROWS), segment_first_row,
        adapter_per_slot.T, adapter_storage_row, frozen_value_weight, slot_down_matrix[0], slot_up_matrix[0],
    )
    state_down = [jax.ShapeDtypeStruct(down_shape, F32)] * 3
    state_up = [jax.ShapeDtypeStruct(up_shape, F32)] * 3
    return pl.pallas_call(
        finish,
        out_shape=(jax.ShapeDtypeStruct((ROWS, WIDTH), BF16), *state_down, *state_up),
        in_specs=[vmem, vmem, hbm, hbm, hbm, vmem, hbm, hbm, hbm],
        out_specs=(hbm,) * 7,
        scratch_shapes=([pltpu.VMEM(down_shape, F32)] * 3 + [pltpu.VMEM(up_shape, F32)] * 3) * 2 + [dma((20,))],
        name="finish",
    )(
        tmp, grad_down, down_matrix_rows, down_first_moment, down_second_moment,
        grad_up, up_matrix_rows, up_first_moment, up_second_moment,
    )


def solution(mesh):
    rows = ("adapter", "tensor")
    stored = P("adapter", None, "tensor")
    in_specs = (
        P(rows, None), P(rows, None), P(rows, None), P(rows), P("adapter", None), P(), P(), P("tensor", None),
        P("adapter", None, None, "tensor"), P("adapter", None, None, None),
        stored, stored, stored, stored, stored, stored,
    )
    out_specs = (P(rows, None),) + (stored,) * 6
    return jax.shard_map(body, mesh=mesh, in_specs=in_specs, out_specs=out_specs, check_vma=False)
```

```python
import jax
import jax.numpy as jnp
from jax import lax
from jax.experimental import pallas as pl
from jax.experimental.pallas import tpu as pltpu
from jax.sharding import PartitionSpec as P

MESH = pl.DeviceIdType.MESH
TILE = 128
STEP = 100
NX, NY, NZ = 4, 4, 8

adapter_scale = 0.5
beta_one = 0.9
beta_two = 0.999
adam_eps = 1e-08
learn_rate = 0.01

ROWS = 256
WIDTH = 8192
KVW = 1024
RANK = 16
SLOTS = 13
TILES = 16
COLS = 1024
UPC = 128
PAY = COLS + UPC
CHUNK = 128
STORED = 4
A, B, C, X, AX, BX, DX = range(7)
CUTS = ((0, 640), (640, PAY))
BLOCK = 256
SUB = 2
VMEM_LIMIT = 58 << 20
SEQ = (
    ("own_y", 0), ("own_x",), ("local",), ("own_y", 1), ("tiles", 0), ("in", X, 1), ("in", A, 0), ("in", X, 0),
    ("in", B, 0), ("in", A, 1), ("in", B, 1), ("tables",), ("in", BX, 0), ("slots", 0), ("tiles", 1),
    ("in", BX, 1), ("in", AX, 1), ("ring", 0, 0), ("in", AX, 0), ("downs",), ("in", B, 2), ("in", X, 2),
    ("in", C, 0), ("slots", 1), ("ring", 0, 1), ("in", A, 3), ("in", A, 2), ("in", B, 3), ("ring", 1, 0),
    ("rest", 1), ("in", C, 1), ("cols", None), ("in", BX, 3), ("ring", 1, 1), ("wait_down",), ("in", X, 3),
    ("in", AX, 2), ("rest", 0), ("in", BX, 2), ("ring", 2, 0), ("in", C, 2), ("cols", X), ("ring", 2, 1),
    ("in", AX, 3), ("cols", BX), ("ring", 3, 0), ("cols", AX), ("in", DX, 0), ("ring", 3, 1), ("in", C, 3),
    ("cols", A), ("in", DX, 1), ("in", DX, 2), ("cols", B), ("in", DX, 3), ("ring", 4, 0), ("cols", C),
    ("ring", 4, 1), ("cols", DX),
)
F32 = jnp.float32
BF16 = jnp.bfloat16


def adam_update(param, first, second, grad):
    first_new = beta_one * first + (1.0 - beta_one) * grad
    second_new = beta_two * second + (1.0 - beta_two) * grad * grad
    bias_one = 1.0 - beta_one**STEP
    bias_two = 1.0 - beta_two**STEP
    moved = first_new / bias_one / (jnp.sqrt(second_new / bias_two) + adam_eps)
    return (param - learn_rate * moved, first_new, second_new)


def kernel(
    acts_h, og_h, midt, rid, seg, apst, stor, w_h, sd_h, su_h,
    out, gd, gu,
    acts, og, sd, su, w, xd, dn,
    gs0, gs1, gr0, gr1, sl0, sl1, dns0, dns1, us0, us1, ur0, ur1, ds0, ds1, dr0, dr1,
    bmt, bm2, tslot, seg2, sr, tab,
    in_sem, w_send, w_recv, sib_recv, dn_send, dn_recv, g_send, g_recv,
    s_send, s_recv, r_send, r_recv, m_sem,
):
    gs, gr, sl, dns = (gs0, gs1), (gr0, gr1), (sl0, sl1), (dns0, dns1)
    us, ur, ds, dr = (us0, us1), (ur0, ur1), (ds0, ds1), (dr0, dr1)
    parts = range(len(CUTS))
    a = lax.axis_index("adapter")
    t = lax.axis_index("tensor")
    z, xh, c = a // 4, (a // 2) % 2, a % 2
    y, xl = t // 2, t % 2
    x = xh * 2 + xl

    def dev(dx=0, dy=0, dz=0, dc=0):
        x_, y_, z_, c_ = (x + dx) % NX, (y + dy) % NY, (z + dz) % NZ, (c + dc) % 2
        return (z_ * 4 + (x_ // 2) * 2 + c_, y_ * 2 + x_ % 2)

    def peer(dy, dx, flip=0):
        return (z * 4 + ((xh + flip) % 2) * 2 + c, ((y + dy) % NY) * 2 + (xl + dx) % 2)

    def tensor_of(dy, dx):
        return ((y + dy) % 4) * 2 + (xl + dx) % 2

    loads = {}
    for i, (name, src, dst) in enumerate(
        (
            ("og", og_h, og),
            ("su", su_h, su),
            ("acts", acts_h, acts),
            ("sd", sd_h, sd),
            ("w", w_h, w.at[t]),
        )
    ):
        loads[name] = pltpu.make_async_copy(src, dst, in_sem.at[i])
        loads[name].start()

    plane = [(2, 1), (2, 0), (1, 1), (3, 1), (0, 1), (1, 0), (3, 0), (0, 0)]
    order = [(dy, dx, flip) for dy, dx in plane for flip in (1, 0)]
    barrier = pltpu.get_barrier_semaphore()
    friends = [peer(*d) for d in order[:-1]] + [dev(dz=1), dev(dz=-1), dev(dc=1)]
    for f in friends:
        pl.semaphore_signal(barrier, inc=1, device_id=f, device_id_type=MESH)

    def tile_slot(j, _):
        n = jnp.int32(-1)
        for k in range(SLOTS):
            n = n + (seg[0, k] <= j * TILE).astype(jnp.int32)
        tslot[j] = n
        return 0

    lax.fori_loop(0, TILES, tile_slot, 0)

    pl.semaphore_wait(barrier, len(friends))

    seg_copy = pltpu.make_async_remote_copy(
        src_ref=seg, dst_ref=seg2, send_sem=m_sem.at[0], recv_sem=m_sem.at[1],
        device_id=peer(0, 0, 1), device_id_type=MESH,
    )
    seg_copy.start()

    e = z % 2
    chunks = (2 * e, 2 * e + 1, 2 * (1 - e), 2 * (1 - e) + 1)
    where = {
        A: tensor_of(1, 0), B: tensor_of(3, 0), C: tensor_of(2, 0), X: tensor_of(0, 1),
        AX: tensor_of(1, 1), BX: tensor_of(3, 1), DX: tensor_of(2, 1),
    }
    sent = []

    def region(piece, chunk, half, sub=None):
        rows = CHUNK if sub is None else CHUNK // SUB
        first = half * 512 + chunk * CHUNK + (0 if sub is None else sub * rows)
        return w.at[piece, pl.ds(pl.multiple_of(first, rows), rows)]

    def push(src, dst, sem, target):
        cp = pltpu.make_async_remote_copy(
            src_ref=src, dst_ref=dst, send_sem=w_send.at[len(sent)], recv_sem=sem, device_id=target, device_id_type=MESH
        )
        cp.start()
        sent.append(cp)

    def push_own(chunk, label, sub, target):
        rows = CHUNK // SUB
        src = w_h.at[pl.ds(pl.multiple_of(c * 512 + chunk * CHUNK + sub * rows, rows), rows)]
        push(src, region(t, chunk, c, sub), w_recv.at[label, chunk, sub], target)

    def sib_arrived(label):
        for chunk in range(4):
            place = region(where[label], chunk, 1 - c)
            pltpu.make_async_copy(place, place, sib_recv.at[label, chunk]).wait()

    up_y, dn_y, up_x, dn_x, up_z, dn_z = dev(dy=1), dev(dy=-1), dev(dx=1), dev(dx=-1), dev(dz=1), dev(dz=-1)

    def own_y(chunk):
        for sub in range(SUB):
            push_own(chunk, B, sub, up_y)
            push_own(chunk, A, sub, dn_y)

    def own_x():
        for sub in range(SUB):
            push_own(chunks[0], X, sub, up_x)
            push_own(chunks[1], X, sub, dn_x)

    def local():
        loads["og"].wait()
        loads["su"].wait()
        kept = []
        bmt[...] = jnp.zeros_like(bmt)
        for i in range(2):
            slot = tslot[2 * t + i]
            ids = rid[:, i * TILE : (i + 1) * TILE]
            prod = lax.dot_general(
                su[slot], og[i * TILE : (i + 1) * TILE], (((1,), (1,)), ((), ())), preferred_element_type=F32
            )
            own = jnp.where(ids == apst[slot, a], adapter_scale * prod, 0.0)
            bmt[i * RANK : (i + 1) * RANK, i * TILE : (i + 1) * TILE] = own.astype(BF16)
            m = midt[:, i * TILE : (i + 1) * TILE]
            kept.append(jnp.where(ids < stor.shape[0], m, jnp.zeros_like(m)))
        bm2[...] = bmt[...].astype(F32).T.astype(BF16)

        loads["acts"].wait()
        for p in parts:
            lo, hi = CUTS[p]
            down = min(hi, COLS) - lo
            if hi > COLS:
                for i in range(2):
                    g = jnp.dot(kept[i], og[i * TILE : (i + 1) * TILE], preferred_element_type=F32)
                    g = (adapter_scale * g).astype(BF16)
                    for u in range(8):
                        gs[p][u, i, :, down:] = g[:, u * UPC : (u + 1) * UPC]
            for u in range(8):
                for i in range(2):
                    block = acts[i * TILE : (i + 1) * TILE, u * COLS + lo : u * COLS + lo + down]
                    low = bmt[i * RANK : (i + 1) * RANK, i * TILE : (i + 1) * TILE]
                    gs[p][u, i, :, :down] = jnp.dot(low, block, preferred_element_type=F32).astype(BF16)

    g_sent = []

    def tiles_out(p):
        for n, (dy, dx, flip) in enumerate(order[:-1]):
            cp = pltpu.make_async_remote_copy(
                src_ref=gs[p].at[tensor_of(dy, dx)], dst_ref=gr[p].at[flip, t],
                send_sem=g_send.at[p, n], recv_sem=g_recv.at[p, n],
                device_id=peer(dy, dx, flip), device_id_type=MESH,
            )
            cp.start()
            g_sent.append(cp)
        gr[p][0, t] = gs[p][t]

    def wait_tiles(p):
        for dy, dx, flip in order[:-1]:
            back = order.index(((4 - dy) % 4, dx, flip))
            place = gr[p].at[flip, tensor_of(dy, dx)]
            pltpu.make_async_copy(place, place, g_recv.at[p, back]).wait()

    dn_sent = []

    def spread(j, _):
        xd[j // 2, pl.ds(pl.multiple_of((j % 2) * RANK, RANK), RANK)] = sd[tslot[j]]
        return 0

    def downs_out():
        loads["sd"].wait()
        lax.fori_loop(0, TILES, spread, 0)
        for n, (dy, dx) in enumerate(plane):
            u = tensor_of(dy, dx)
            if (dy, dx) == (0, 0):
                dn[t] = xd[t]
            else:
                cp = pltpu.make_async_remote_copy(
                    src_ref=xd.at[u], dst_ref=dn.at[t], send_sem=dn_send.at[n], recv_sem=dn_recv.at[n],
                    device_id=peer(dy, dx), device_id_type=MESH,
                )
                cp.start()
                dn_sent.append(cp)

    def wait_down():
        for dy, dx in plane[:-1]:
            place = dn.at[tensor_of(dy, dx)]
            pltpu.make_async_copy(place, place, dn_recv.at[plane.index(((4 - dy) % 4, dx))]).wait()

    def in_grad(piece):
        for j in range(COLS // BLOCK):
            rows = pl.ds(j * BLOCK, BLOCK)
            cols = pl.ds(pl.multiple_of(piece * COLS + j * BLOCK, BLOCK), BLOCK)
            full = lax.dot_general(og[...], w[piece, rows], (((1,), (1,)), ((), ())), preferred_element_type=F32)
            low = jnp.dot(bm2[...], dn[piece, :, rows], preferred_element_type=F32)
            out[:, cols] = (full + low).astype(BF16)

    def find(n, _):
        q, rest = n // 32, n % 32
        row = ((z + rest // 4) % NZ) * 16 + xh * 8 + c * 4 + rest % 4
        k_found = jnp.int32(0)
        for k in range(SLOTS):
            k_found = jnp.where(sr[q * SLOTS + k] == row, k + 1, k_found)
        tab[n] = k_found
        return 0

    def tables():
        for q in range(4):
            group = z * 4 + (xh ^ (q % 2)) * 2 + (c ^ (q // 2))
            for k in range(SLOTS):
                sr[q * SLOTS + k] = stor[apst[k, group]]
        lax.fori_loop(0, 128, find, 0)

    s_sent = []

    def slots_out(p):
        if p == 0:
            seg_copy.wait()
        wait_tiles(p)
        for q, table in ((0, seg), (1, seg2)):
            for k in range(SLOTS):
                first = table[0, k] // TILE
                last = table[0, k + 1] // TILE if k + 1 < SLOTS else TILES
                total = jnp.zeros((RANK, sl[p].shape[-1]), F32)
                for i in range(4):
                    j = jnp.minimum(first + i, TILES - 1)
                    total = total + jnp.where(first + i < last, gr[p][q, j // 2, j % 2].astype(F32), 0.0)
                sl[p][q, k] = total.astype(BF16)
        cp = pltpu.make_async_remote_copy(
            src_ref=sl[p].at[pl.ds(0, 2)], dst_ref=sl[p].at[pl.ds(2, 2)], send_sem=s_send.at[p], recv_sem=s_recv.at[p],
            device_id=dev(dc=1), device_id_type=MESH,
        )
        cp.start()
        s_sent.append(cp)

    def gather_rows(p, dz):
        def one(r, _):
            total = jnp.zeros((RANK, sl[p].shape[-1]), F32)
            for q in range(4):
                k = tab[q * 32 + dz * 4 + r]
                total = total + jnp.where(k > 0, sl[p][q, jnp.maximum(k - 1, 0)].astype(F32), 0.0)
            dns[p][dz, r] = total
            return 0

        lax.fori_loop(0, STORED, one, 0)

    r_sent = []

    def ring_send(src, dst, p, direction, step):
        n = direction * 4 + step
        cp = pltpu.make_async_remote_copy(
            src_ref=src, dst_ref=dst, send_sem=r_send.at[p, n], recv_sem=r_recv.at[p, n],
            device_id=dn_z if direction else up_z, device_id_type=MESH,
        )
        cp.start()
        r_sent.append(cp)

    def ring_wait(ref, p, direction, step):
        pltpu.make_async_copy(ref, ref, r_recv.at[p, direction * 4 + step]).wait()

    def ring(step, p):
        if step == 0:
            place = sl[p].at[pl.ds(2, 2)]
            pltpu.make_async_copy(place, place, s_recv.at[p]).wait()
            gather_rows(p, 4)
            us[p][0, 0:2] = dns[p][4, 0:2].astype(BF16)
            ring_send(us[p].at[0, pl.ds(0, 2)], ur[p].at[0, pl.ds(0, 2)], p, 0, 0)
            ds[p][0, 2:4] = dns[p][4, 2:4].astype(BF16)
            ring_send(ds[p].at[0, pl.ds(2, 2)], dr[p].at[0, pl.ds(2, 2)], p, 1, 0)
            gather_rows(p, 3)
            gather_rows(p, 5)
        elif step == 1:
            ring_wait(ur[p].at[0, pl.ds(0, 2)], p, 0, 0)
            us[p][1, 0:2] = (dns[p][3, 0:2] + ur[p][0, 0:2].astype(F32)).astype(BF16)
            us[p][1, 2:4] = dns[p][3, 2:4].astype(BF16)
            ring_send(us[p].at[1], ur[p].at[1], p, 0, 1)
            ring_wait(dr[p].at[0, pl.ds(2, 2)], p, 1, 0)
            ds[p][1, 0:2] = dns[p][5, 0:2].astype(BF16)
            ds[p][1, 2:4] = (dns[p][5, 2:4] + dr[p][0, 2:4].astype(F32)).astype(BF16)
            ring_send(ds[p].at[1], dr[p].at[1], p, 1, 1)
        elif step < 4:
            ring_wait(ur[p].at[step - 1], p, 0, step - 1)
            us[p][step] = (dns[p][4 - step] + ur[p][step - 1].astype(F32)).astype(BF16)
            ring_send(us[p].at[step], ur[p].at[step], p, 0, step)
            ring_wait(dr[p].at[step - 1], p, 1, step - 1)
            ds[p][step] = (dns[p][4 + step] + dr[p][step - 1].astype(F32)).astype(BF16)
            ring_send(ds[p].at[step], dr[p].at[step], p, 1, step)
        else:
            ring_wait(ur[p].at[3], p, 0, 3)
            ring_wait(dr[p].at[3], p, 1, 3)
            total = dns[p][0] + ur[p][3].astype(F32) + dr[p][3].astype(F32)
            lo, hi = CUTS[p]
            down = min(hi, COLS) - lo
            gd[:, :, lo : lo + down] = total[:, :, :down]
            if hi > COLS:
                gu[...] = total[:, :, down:]

    def gather_rest(p):
        for dz in (2, 6, 1, 7, 0):
            gather_rows(p, dz)

    passing = {
        (A, 0): ((C, dn_y), (AX, up_x), (A, up_z)),
        (A, 1): ((AX, dn_x), (A, dn_z)),
        (A, 2): ((C, dn_y),),
        (B, 0): ((BX, dn_x), (B, dn_z)),
        (B, 1): ((C, up_y), (BX, up_x), (B, up_z)),
        (B, 3): ((C, up_y),),
        (X, 0): ((X, up_z),),
        (X, 1): ((X, dn_z),),
        (AX, 0): ((AX, up_z),),
        (AX, 1): ((AX, dn_z),),
        (BX, 0): ((BX, dn_z),),
        (BX, 1): ((BX, up_z),),
        (C, 0): ((DX, up_x),),
        (C, 1): ((DX, dn_x),),
        (AX, 2): ((DX, dn_y),),
        (BX, 3): ((DX, up_y),),
    }

    def chunk_in(label, n):
        for sub in range(SUB):
            place = region(where[label], chunks[n], c, sub)
            pltpu.make_async_copy(place, place, w_recv.at[label, chunks[n], sub]).wait()
            for new, target in passing.get((label, n), ()):
                push(place, place, w_recv.at[new, chunks[n], sub], target)
        place = region(where[label], chunks[n], c)
        push(place, place, sib_recv.at[label, chunks[n]], dev(dc=1))

    def columns(label):
        if label is None:
            loads["w"].wait()
            in_grad(t)
        else:
            sib_arrived(label)
            in_grad(where[label])

    steps = {
        "local": local,
        "own_y": lambda n: own_y(chunks[n]),
        "own_x": own_x,
        "tiles": tiles_out,
        "downs": downs_out,
        "tables": tables,
        "slots": slots_out,
        "ring": ring,
        "rest": gather_rest,
        "in": chunk_in,
        "cols": columns,
        "wait_down": wait_down,
    }
    for name, *arg in SEQ:
        steps[name](*arg)

    for cp in sent + g_sent + dn_sent + s_sent + r_sent:
        cp.wait_send()


def finish(tmp, grad_down, *refs):
    states, grad_up, outs, bufs, sems = refs[:3], refs[3], refs[7:14], refs[14:26], refs[26]
    states += refs[4:7]
    loads = [pltpu.make_async_copy(states[i], bufs[i], sems.at[i]) for i in range(6)]
    for cp in loads:
        cp.start()
    moves = []

    def leave(src, dst):
        cp = pltpu.make_async_copy(src, dst, sems.at[6 + len(moves)])
        cp.start()
        moves.append(cp)

    step = ROWS // 8
    for i in range(8):
        rows = pl.ds(i * step, step)
        leave(tmp.at[rows], outs[0].at[rows])
    for cp in loads:
        cp.wait()
    for half, grad in enumerate((grad_down, grad_up)):
        new = adam_update(*(ref[...] for ref in bufs[half * 3 : half * 3 + 3]), grad[...])
        for i in range(3):
            n = half * 3 + i
            bufs[6 + n][...] = new[i]
            leave(bufs[6 + n], outs[1 + n])
    for cp in moves:
        cp.wait()


def body(
    acts, output_gradient, adapter_middle_saved, adapter_per_row, segment_first_row, adapter_per_slot,
    adapter_storage_row, frozen_value_weight, slot_down_matrix, slot_up_matrix, down_matrix_rows,
    down_first_moment, down_second_moment, up_matrix_rows, up_first_moment, up_second_moment,
):
    vmem = pl.BlockSpec(memory_space=pltpu.VMEM)
    smem = pl.BlockSpec(memory_space=pltpu.SMEM)
    hbm = pl.BlockSpec(memory_space=pl.ANY)
    dma = pltpu.SemaphoreType.DMA
    widths = [hi - lo for lo, hi in CUTS]
    n = len(CUTS)

    def each(shape, dtype):
        return [pltpu.VMEM((*shape, width), dtype) for width in widths]

    down_shape, up_shape = (STORED, RANK, COLS), (STORED, RANK, UPC)
    tmp, grad_down, grad_up = pl.pallas_call(
        kernel,
        out_shape=(
            pltpu.VMEM((ROWS, WIDTH), BF16),
            pltpu.VMEM(down_shape, F32),
            pltpu.VMEM(up_shape, F32),
        ),
        in_specs=[hbm, hbm, vmem, vmem, smem, smem, smem, hbm, hbm, hbm],
        out_specs=(vmem, vmem, vmem),
        scratch_shapes=[
            pltpu.VMEM((ROWS, WIDTH), BF16),
            pltpu.VMEM((ROWS, KVW), BF16),
            pltpu.VMEM((SLOTS, RANK, COLS), BF16),
            pltpu.VMEM((SLOTS, RANK, KVW), BF16),
            pltpu.VMEM((8, COLS, KVW), BF16),
            pltpu.VMEM((8, 2 * RANK, COLS), BF16),
            pltpu.VMEM((8, 2 * RANK, COLS), BF16),
            *each((8, 2, RANK), BF16),
            *each((2, 8, 2, RANK), BF16),
            *each((4, SLOTS, RANK), BF16),
            *each((NZ, STORED, RANK), F32),
            *each((4, STORED, RANK), BF16),
            *each((4, STORED, RANK), BF16),
            *each((4, STORED, RANK), BF16),
            *each((4, STORED, RANK), BF16),
            pltpu.VMEM((2 * RANK, ROWS), BF16),
            pltpu.VMEM((ROWS, 2 * RANK), BF16),
            pltpu.SMEM((TILES,), jnp.int32),
            pltpu.SMEM((1, SLOTS), jnp.int32),
            pltpu.SMEM((4 * SLOTS,), jnp.int32),
            pltpu.SMEM((128,), jnp.int32),
            dma((5,)),
            dma((28 * (SUB + 1),)),
            dma((7, 4, SUB)),
            dma((7, 4)),
            dma((7,)),
            dma((7,)),
            dma((n, 15)),
            dma((n, 15)),
            dma((n,)),
            dma((n,)),
            dma((n, 8)),
            dma((n, 8)),
            dma((2,)),
        ],
        compiler_params=pltpu.CompilerParams(collective_id=0, has_side_effects=True, vmem_limit_bytes=VMEM_LIMIT),
        cost_estimate=pl.CostEstimate(flops=2 * ROWS * WIDTH * KVW, bytes_accessed=12 << 20, transcendentals=0),
        name="fused",
    )(
        acts, output_gradient, adapter_middle_saved.T, adapter_per_row.reshape(1, ROWS), segment_first_row,
        adapter_per_slot.T, adapter_storage_row, frozen_value_weight, slot_down_matrix[0], slot_up_matrix[0],
    )
    state_down = [jax.ShapeDtypeStruct(down_shape, F32)] * 3
    state_up = [jax.ShapeDtypeStruct(up_shape, F32)] * 3
    return pl.pallas_call(
        finish,
        out_shape=(jax.ShapeDtypeStruct((ROWS, WIDTH), BF16), *state_down, *state_up),
        in_specs=[vmem, vmem, hbm, hbm, hbm, vmem, hbm, hbm, hbm],
        out_specs=(hbm,) * 7,
        scratch_shapes=([pltpu.VMEM(down_shape, F32)] * 3 + [pltpu.VMEM(up_shape, F32)] * 3) * 2 + [dma((20,))],
        compiler_params=pltpu.CompilerParams(vmem_limit_bytes=8 << 20),
        name="finish",
    )(
        tmp, grad_down, down_matrix_rows, down_first_moment, down_second_moment,
        grad_up, up_matrix_rows, up_first_moment, up_second_moment,
    )


def solution(mesh):
    rows = ("adapter", "tensor")
    stored = P("adapter", None, "tensor")
    in_specs = (
        P(rows, None), P(rows, None), P(rows, None), P(rows), P("adapter", None), P(), P(), P("tensor", None),
        P("adapter", None, None, "tensor"), P("adapter", None, None, None),
        stored, stored, stored, stored, stored, stored,
    )
    out_specs = (P(rows, None),) + (stored,) * 6
    return jax.shard_map(body, mesh=mesh, in_specs=in_specs, out_specs=out_specs, check_vma=False)
```
